256 devices in a mesh: row: 64 (over y, x_lo, z), col: 4 (over x_hi, core).
Axes of the slice: x: 4 (x_hi: 2, x_lo: 2; x = x_hi * 2 + x_lo), y: 4, z: 8, core: 2. Of those that a mesh axis runs over, the one named last changes fastest.
Arguments:
- features: bfloat16 [32768, 256], P(('row', 'col')), may hold values from -6 to 6
- degree: int32 [32768], P(('row', 'col')), may hold values from 16 to 64
- tile_count: int32 [4, 64], P('col', 'row'), may hold values from 1 to 256, 6553 in all within a row
- tile_rows: int32 [4, 64, 256], P('col', 'row'), may hold values from 0 to 3
- tile_cols: int32 [4, 64, 256], P('col', 'row'), may hold values from 0 to 63
- tile_values: bfloat16 [4, 64, 256, 128, 128], P('col', 'row'), may hold values from 0 to 1
- w_self: bfloat16 [256, 256], replicated, may hold values from -0.375 to 0.375
- w_neigh: bfloat16 [256, 256], replicated, may hold values from -0.375 to 0.375
- bias_term: float32 [256], replicated, may hold values from -3 to 3
- grad_out: bfloat16 [32768, 256], P(('row', 'col')), may hold values from -6 to 6
Outputs:
- layer_out: bfloat16 [32768, 256], P(('row', 'col'))
- grad_input: bfloat16 [32768, 256], P(('row', 'col'))
- grad_self: float32 [256, 256], replicated
- grad_neigh: float32 [256, 256], replicated
- grad_bias: float32 [256], replicated
The draws below stay inside these ranges and needn't reach their ends.
Inputs may be any that keep to these rules, and one draw needn't show every extreme that they name: `tile_count`: in every column group c some device holds exactly 256 live tiles; slots at or past a device's count are unused.
All inputs are finite; a program needn't handle non-finite values.
Results may differ from the reference program's by a relative error of at most 0.007.
Values may be sent and summed in bfloat16 or wider, within the bound.
No kernel may reach another device: no remote copies, remote signals or barrier semaphores. Data moves between devices by JAX's collectives and lax.ppermute only.
A program may use at most 128 MiB of HBM per device.

```python
import math
import jax
import jax.numpy as jnp
import numpy as np
from jax import lax

F = 256
TILE = 128
NODE_DEV = 128
CAP = 256
NODES = 32768
ROW_TILES = 4
COL_TILES = 64
N_ROW = 64
N_COL = 4


def place_ends(array, own_key, smallest, top_value):
    longest = array.shape.index(max(array.shape))
    spots = []
    for shift in (0, 1):
        where = [jax.random.randint(jax.random.fold_in(own_key, axis), (), 0, length) for axis, length in enumerate(array.shape)]
        where[longest] = (where[longest] + shift) % array.shape[longest]
        spots.append(tuple(where))
    return array.at[spots[0]].set(smallest).at[spots[1]].set(top_value)


def levels(own_key, shape, split, least, top_value):
    def one(dim, blocks):
        steps = jax.random.uniform(jax.random.fold_in(jax.random.fold_in(own_key, 6), dim), (blocks,), jnp.float32, least / len(split), top_value / len(split))
        return jnp.repeat(jnp.exp(steps), shape[dim] // blocks).reshape((-1,) + (1,) * (len(shape) - dim - 1))

    factor_of = one(*split[0])
    for cut in split[1:]:
        factor_of = factor_of * one(*cut)
    return factor_of


def profile(amount, total, most, slope):
    weights = [(1 << 20) // math.isqrt(grade ** slope) + 1 for grade in range(2, amount + 1)]
    rest, holding = total - most - (amount - 1), [1] * (amount - 1)
    while rest > 0:
        movable = [i for i in range(amount - 1) if holding[i] < most]
        pool, budget = sum([weights[i] for i in movable]), rest
        for i in movable:
            extra = min(most - holding[i], max(1, budget * weights[i] // pool), rest)
            holding[i] = holding[i] + extra
            rest = rest - extra
    return np.array([most] + holding)


def uneven_parts(own_key, amount, total, reach, skew):
    if amount == 2:
        one = jax.random.randint(own_key, (), max(1, total - reach), min(reach, total - 1) + 1)
        return jnp.stack([one, total - one])
    lengths = jnp.asarray(profile(amount, total, reach, skew), jnp.int32)
    twos = (amount - 1) // 2
    donor, receiver = lengths[1:1 + 2 * twos:2], lengths[2:2 + 2 * twos:2]
    room = jnp.minimum(donor - 1, reach - receiver)
    passed = jax.random.randint(jax.random.fold_in(own_key, 1), (twos,), 0, 1 << 20) % (room + 1)
    lengths = lengths.at[1:1 + 2 * twos:2].set(donor - passed).at[2:2 + 2 * twos:2].set(receiver + passed)
    return lengths[jax.random.permutation(jax.random.fold_in(own_key, 2), amount)]


def scatter_about(stream_key, shape, deviation, bound, pieces=(), held_as=jnp.bfloat16):
    gain = levels(stream_key, shape, pieces, -0.22, 0.18) if pieces else 1.0
    result = jax.random.normal(stream_key, shape, jnp.float32) * deviation * gain
    return jnp.minimum(jnp.maximum(result, -bound), bound).astype(held_as)


def setup_inputs(seed: int = 0) -> dict:
    key_list = jax.random.split(jax.random.key(seed), 11)
    return {
        "features": scatter_about(key_list[0], (NODES, F), 1.0, 6.0, ((0, 256),)),
        "degree": place_ends(jax.random.randint(key_list[1], (NODES,), 16, 65), jax.random.fold_in(key_list[1], 1), 16, 64).astype(jnp.int32),
        "tile_count": jax.vmap(lambda own: uneven_parts(own, N_ROW, N_ROW * CAP * 2 // 5, CAP, 2))(jax.random.split(key_list[2], N_COL)).reshape((N_COL, N_ROW)).astype(jnp.int32),
        "tile_rows": place_ends(jax.random.randint(key_list[3], (N_COL, N_ROW, CAP), 0, ROW_TILES), jax.random.fold_in(key_list[3], 1), 0, ROW_TILES - 1).astype(jnp.int32),
        "tile_cols": place_ends(jax.random.randint(key_list[4], (N_COL, N_ROW, CAP), 0, COL_TILES), jax.random.fold_in(key_list[4], 1), 0, COL_TILES - 1).astype(jnp.int32),
        "tile_values": jnp.clip(1.0 * jax.random.uniform(key_list[5], (N_COL, N_ROW, CAP, TILE, TILE), jnp.float32) ** levels(key_list[5], (N_COL, N_ROW, CAP, TILE, TILE), ((0, 4), (1, 64)), -0.2, 0.2), 0.0, 1.0).astype(jnp.bfloat16),
        "w_self": scatter_about(key_list[6], (F, F), F ** -0.5, 0.375),
        "w_neigh": scatter_about(key_list[7], (F, F), F ** -0.5, 0.375),
        "bias_term": scatter_about(key_list[8], (F,), 0.5, 3.0, (), jnp.float32),
        "grad_out": scatter_about(key_list[9], (NODES, F), 1.0, 6.0, ((0, 256),)),
    }


def gather_rows(blocks, row_ids, col_ids, values, live_slots, running):
    group_size = math.gcd(32, row_ids.shape[0])
    row_tiles = running.shape[0]

    def advance(turn_index, running):
        offset = turn_index * group_size
        row_pick = lax.dynamic_slice_in_dim(row_ids, offset, group_size)
        col_pick = lax.dynamic_slice_in_dim(col_ids, offset, group_size)
        weights = lax.dynamic_slice_in_dim(values, offset, group_size, 0).astype(jnp.float32)
        usable = (offset + jnp.arange(group_size, dtype=jnp.int32) < live_slots).astype(jnp.float32)
        inputs = blocks[col_pick].astype(jnp.float32)
        products = jnp.einsum('gik,gkf->gif', weights, inputs, precision=lax.Precision.HIGHEST)
        selector = (row_pick[:, None] == jnp.arange(row_tiles, dtype=jnp.int32)[None, :]).astype(jnp.float32) * usable[:, None]
        return running + jnp.einsum('gr,gif->rif', selector, products, precision=lax.Precision.HIGHEST)
    turn_total = (live_slots + group_size - 1) // group_size
    return lax.fori_loop(0, turn_total, advance, running)

def spread_columns(sources, row_ids, col_ids, values, live_slots, running):
    group_size = math.gcd(32, row_ids.shape[0])

    def advance(turn_index, running):
        offset = turn_index * group_size
        row_pick = lax.dynamic_slice_in_dim(row_ids, offset, group_size)
        col_pick = lax.dynamic_slice_in_dim(col_ids, offset, group_size)
        weights = lax.dynamic_slice_in_dim(values, offset, group_size, 0).astype(jnp.float32)
        usable = (offset + jnp.arange(group_size, dtype=jnp.int32) < live_slots).astype(jnp.float32)
        inputs = sources[row_pick].astype(jnp.float32)
        products = jnp.einsum('gik,gif->gkf', weights, inputs, precision=lax.Precision.HIGHEST) * usable[:, None, None]
        return running.at[col_pick].add(products)
    turn_total = (live_slots + group_size - 1) // group_size
    return lax.fori_loop(0, turn_total, advance, running)

def reference(features, degree, tile_count, tile_rows, tile_cols, tile_values, w_self, w_neigh, bias_term, grad_out):
    node_blocks = features.reshape(N_ROW, N_COL, NODE_DEV, F)
    agg_sum = jnp.zeros((NODES, F), jnp.float32)
    for column in range(N_COL):
        blocks = node_blocks[:, column].reshape(COL_TILES, TILE, F)

        def row_group(row_index):
            running = jnp.zeros((ROW_TILES, TILE, F), jnp.float32)
            return gather_rows(blocks, tile_rows[column][row_index], tile_cols[column][row_index], tile_values[column][row_index], tile_count[column][row_index], running)
        agg_sum = agg_sum + lax.map(row_group, jnp.arange(N_ROW, dtype=jnp.int32)).reshape(NODES, F)
    divisor = degree[:, None].astype(jnp.float32)
    aggregate = (agg_sum / divisor).astype(jnp.bfloat16)
    pre_act = jnp.dot(features, w_self, preferred_element_type=jnp.float32) + jnp.dot(aggregate, w_neigh, preferred_element_type=jnp.float32) + bias_term
    sigmoid_pre = jax.nn.sigmoid(pre_act)
    layer_out = (pre_act * sigmoid_pre).astype(jnp.bfloat16)
    grad_pre = (grad_out.astype(jnp.float32) * (sigmoid_pre * (1.0 + pre_act * (1.0 - sigmoid_pre)))).astype(jnp.bfloat16)
    norm_scale = 1.0 / math.sqrt(NODES)
    grad_self = jnp.dot(features.T, grad_pre, preferred_element_type=jnp.float32) * norm_scale
    grad_neigh = jnp.dot(aggregate.T, grad_pre, preferred_element_type=jnp.float32) * norm_scale
    grad_bias = lax.optimization_barrier(jnp.sum(grad_pre.astype(jnp.float32), axis=0)) * norm_scale
    scaled_grad = (jnp.dot(grad_pre, w_neigh.T, preferred_element_type=jnp.float32) / divisor).astype(jnp.bfloat16)
    grad_rows = scaled_grad.reshape(N_ROW, ROW_TILES, TILE, F)
    columns_out = []
    for column in range(N_COL):

        def row_step(running, row_index):
            return (spread_columns(grad_rows[row_index], tile_rows[column][row_index], tile_cols[column][row_index], tile_values[column][row_index], tile_count[column][row_index], running), None)
        running, unused = lax.scan(row_step, jnp.zeros((COL_TILES, TILE, F), jnp.float32), jnp.arange(N_ROW, dtype=jnp.int32))
        columns_out.append(running.reshape(N_ROW, NODE_DEV, F))
    neighbor_back = jnp.stack(columns_out, axis=1).reshape(NODES, F)
    grad_input = (jnp.dot(grad_pre, w_self.T, preferred_element_type=jnp.float32) + neighbor_back).astype(jnp.bfloat16)
    return (layer_out, grad_input, grad_self, grad_neigh, grad_bias)
```

```python
import functools
import math

import jax
import jax.numpy as jnp
from jax import lax
from jax.experimental import pallas as pl
from jax.experimental.pallas import tpu as pltpu
from jax.sharding import PartitionSpec as P

NY, NX, NZ, NC = 4, 2, 8, 4
TILE = 128
RING = 16
bf16, f32 = jnp.bfloat16, jnp.float32


def row_id(y, x, z):
    return (y % NY * NX + x % NX) * NZ + z % NZ


def row_perm(move):
    return [
        (row_id(y, x, z), row_id(*move(y, x, z)))
        for y in range(NY)
        for x in range(NX)
        for z in range(NZ)
    ]


def shift_z(a, d):
    return lax.ppermute(a, "row", row_perm(lambda y, x, z: (y, x, z + d)))


def shift_y(a, d):
    return lax.ppermute(a, "row", row_perm(lambda y, x, z: (y + d, x, z)))


def swap_x(a):
    return lax.ppermute(a, "row", row_perm(lambda y, x, z: (y, 1 - x, z)))


def swap_bits(a, name, size, bit):
    return lax.ppermute(a, name, [(i, i ^ bit) for i in range(size)])


def swap_col(a, bit):
    return swap_bits(a, "col", NC, bit)


def ring_place(step, n):
    return jnp.where(step < n // 2, 2 * step, jnp.where(step == n // 2, n - 1, 2 * (n - step) - 1))


def plan_tiles(tile_count, tile_rows, tile_cols):
    r, c = lax.axis_index("row"), lax.axis_index("col")
    z, x, y = r % NZ, r // NZ % NX, r // (NZ * NX)
    count, rows, cols = tile_count[0, 0], tile_rows[0, 0], tile_cols[0, 0]
    zi = ring_place((cols % NZ - z) % NZ, NZ)
    yi = ring_place((cols // (NZ * NX) - y) % NY, NY)
    place = jnp.where(cols // NZ % NX == 0, yi * NZ + zi, NY * NZ + zi * NY + yi)
    slots = jnp.arange(rows.shape[0], dtype=jnp.int32)
    quarter = jnp.where(slots < count, place // 16, 4)
    packed = slots * 64 + (rows ^ c) * 16 + place % 16
    before = (quarter[None, :] < quarter[:, None]) | (
        (quarter[None, :] == quarter[:, None]) & (slots[None, :] < slots[:, None])
    )
    rank = jnp.sum(before.astype(jnp.int32), axis=1)
    listed = jnp.sum(jnp.where(rank[:, None] == slots[None, :], packed[:, None], 0), axis=0)
    starts = jnp.sum((quarter[None, :] < jnp.arange(8, dtype=jnp.int32)[:, None]).astype(jnp.int32), axis=1)
    return starts, listed


def dense_kernel(part, starts, listed, values, *rest):
    outs, (sums, ring, sems) = rest[:-3], rest[-3:]
    first = starts[part]
    amount = starts[part + 1] - first

    def fetch(j):
        slot = listed[first + j] // 64
        b = lax.rem(j, RING)
        return pltpu.make_async_copy(values.at[slot], ring.at[b], sems.at[b])

    for b in range(RING):

        @pl.when(b < amount)
        def _():
            fetch(b).start()

    def clear(i, carry):
        sums[i] = jnp.zeros((TILE, TILE), f32)
        return carry

    lax.fori_loop(0, 64, clear, 0)

    def add(j, carry):
        fetch(j).wait()
        cell = lax.rem(listed[first + j], 64)
        sums[cell] += ring[lax.rem(j, RING)].astype(f32)

        @pl.when(j + RING < amount)
        def _():
            fetch(j + RING).start()

        return carry

    lax.fori_loop(0, amount, add, 0)
    per = 16 // len(outs)
    for n, out in enumerate(outs):
        for u in range(NC):
            for j in range(per):
                out[u * TILE : (u + 1) * TILE, j * TILE : (j + 1) * TILE] = sums[
                    u * 16 + n * per + j
                ].astype(bf16)


def dense_part(part, starts, listed, values):
    pieces = 2 if part < 2 else 4
    return pl.pallas_call(
        functools.partial(dense_kernel, part),
        out_shape=[jax.ShapeDtypeStruct((NC * TILE, 16 // pieces * TILE), bf16)] * pieces,
        in_specs=[
            pl.BlockSpec(memory_space=pltpu.SMEM),
            pl.BlockSpec(memory_space=pltpu.SMEM),
            pl.BlockSpec(memory_space=pl.ANY),
        ],
        out_specs=[pl.BlockSpec(memory_space=pltpu.VMEM)] * pieces,
        scratch_shapes=[
            pltpu.VMEM((64, TILE, TILE), f32),
            pltpu.VMEM((RING, TILE, TILE), bf16),
            pltpu.SemaphoreType.DMA((RING,)),
        ],
        compiler_params=pltpu.CompilerParams(vmem_limit_bytes=16 * 2**20),
        cost_estimate=pl.CostEstimate(flops=4 * 10**6, bytes_accessed=8 * 2**20, transcendentals=0),
        name=f"dense{part}",
    )(starts, listed, values)


def gather_ring(block, shift, n):
    half = block.shape[0] // 2
    got = [block]
    down = up = block
    for _ in range(n // 2 - 1):
        down, up = shift(down, 1), shift(up, -1)
        got += [down, up]
    got.append((shift(down[:half], 1), shift(up[half:], -1)))
    return got


def joined(parts):
    flat = []
    for part in parts:
        flat += list(part) if isinstance(part, tuple) else [part]
    return flat


def reduce_ring(terms, shift, n, send):
    half = terms[0].shape[0] // 2
    far = terms[n - 1]
    down, up = shift(far[:half].astype(send), 1), shift(far[half:].astype(send), -1)
    for step in range(n // 2 - 1, 0, -1):
        plus, minus = terms[2 * step], terms[2 * step - 1]
        if step == n // 2 - 1:
            down = (
                shift((plus[:half] + down.astype(f32)).astype(send), 1),
                shift(plus[half:].astype(send), 1),
            )
            up = (
                shift(minus[:half].astype(send), -1),
                shift((minus[half:] + up.astype(f32)).astype(send), -1),
            )
        else:
            down = tuple(
                shift((t + d.astype(f32)).astype(send), 1)
                for t, d in zip((plus[:half], plus[half:]), down)
            )
            up = tuple(
                shift((t + d.astype(f32)).astype(send), -1)
                for t, d in zip((minus[:half], minus[half:]), up)
            )
    own = terms[0]
    return jnp.concatenate(
        [
            t + a.astype(f32) + b.astype(f32)
            for t, a, b in zip((own[:half], own[half:]), down, up)
        ],
        axis=0,
    )


def dot(a, b):
    return jnp.dot(a, b, preferred_element_type=f32)


def dot_t(a, b):
    return lax.dot_general(a, b, (((0,), (0,)), ((), ())), preferred_element_type=f32)


def shards(
    features,
    degree,
    tile_count,
    tile_rows,
    tile_cols,
    tile_values,
    w_self,
    w_neigh,
    bias_term,
    grad_out,
):
    r, c = lax.axis_index("row"), lax.axis_index("col")
    x = r // NZ % NX
    nodes = features.shape[0]
    node_total = nodes * NY * NX * NZ * NC

    starts, listed = plan_tiles(tile_count, tile_rows, tile_cols)
    dense = [dense_part(part, starts, listed, tile_values[0, 0]) for part in range(4)]
    dense_y = [*dense[0], *dense[1]]
    dense_z = [*dense[2], *dense[3]]

    other = swap_x(features)
    block0 = jnp.where(x == 0, features, other)
    block1 = jnp.where(x == 0, other, features)
    line_z = jnp.concatenate(joined(gather_ring(block0, shift_z, NZ)), axis=0)
    line_y = jnp.concatenate(joined(gather_ring(block1, shift_y, NY)), axis=0)
    plane_zy = gather_ring(line_z, shift_y, NY)
    plane_yz = gather_ring(line_y, shift_z, NZ)

    partial_sum = jnp.zeros((NC * TILE, features.shape[1]), f32)
    for a, b in zip(dense_y + dense_z, plane_zy + plane_yz):
        b = jnp.concatenate(b, axis=0) if isinstance(b, tuple) else b
        partial_sum = partial_sum + dot(a, b)

    agg_sum = partial_sum[:nodes]
    for k in range(1, NC):
        agg_sum = agg_sum + swap_col(partial_sum[k * nodes : (k + 1) * nodes], k)

    divisor = degree[:, None].astype(f32)
    aggregate = (agg_sum / divisor).astype(bf16)
    pre_act = dot(features, w_self) + dot(aggregate, w_neigh) + bias_term
    sigmoid_pre = jax.nn.sigmoid(pre_act)
    layer_out = (pre_act * sigmoid_pre).astype(bf16)
    grad_pre = (
        grad_out.astype(f32) * (sigmoid_pre * (1.0 + pre_act * (1.0 - sigmoid_pre)))
    ).astype(bf16)
    scaled_grad = (dot(grad_pre, w_neigh.T) / divisor).astype(bf16)

    row_grads = jnp.concatenate(
        [scaled_grad] + [swap_col(scaled_grad, k) for k in range(1, NC)], axis=0
    )

    terms_y = [dot_t(a, row_grads) for a in dense_y]
    terms_z = [dot_t(a, row_grads) for a in dense_z]
    line_z = reduce_ring(terms_y, shift_y, NY, bf16)
    line_y = reduce_ring(terms_z, shift_z, NZ, bf16)
    sum0 = reduce_ring([line_z[i * nodes : (i + 1) * nodes] for i in range(NZ)], shift_z, NZ, bf16)
    sum1 = reduce_ring([line_y[i * nodes : (i + 1) * nodes] for i in range(NY)], shift_y, NY, bf16)
    kept = jnp.where(x == 0, sum0, sum1)
    sent = jnp.where(x == 0, sum1, sum0)
    neighbor_back = kept + swap_x(sent.astype(bf16)).astype(f32)
    grad_input = (dot(grad_pre, w_self.T) + neighbor_back).astype(bf16)

    norm_scale = 1.0 / math.sqrt(node_total)
    local = jnp.concatenate([dot_t(features, grad_pre), dot_t(aggregate, grad_pre)], axis=0) * norm_scale
    local_bias = jnp.sum(grad_pre.astype(f32), axis=0, keepdims=True) * norm_scale
    local_bias = jnp.pad(local_bias, ((0, 7), (0, 0)))

    def share(k):
        part = lax.dynamic_slice_in_dim(local, (c ^ k) * nodes, nodes, axis=0)
        return jnp.concatenate([part, local_bias], axis=0)

    got = [share(0)] + [swap_col(share(k), k) for k in range(1, NC)]
    total = (got[0] + got[1]) + (got[2] + got[3])
    for bit in (1, 2, 4, 16, 32, 8):
        total = total + swap_bits(total, "row", NY * NX * NZ, bit)
    quarters = jnp.stack([total[:nodes]] + [swap_col(total[:nodes], k) for k in range(1, NC)])
    grads = quarters[c ^ jnp.arange(NC, dtype=jnp.int32)].reshape(NC * nodes, -1)
    width = features.shape[1]
    return (layer_out, grad_input, grads[:width], grads[width:], total[nodes])


def solution(mesh):
    return jax.shard_map(
        shards,
        mesh=mesh,
        in_specs=(
            P(("row", "col"), None),
            P(("row", "col")),
            P("col", "row"),
            P("col", "row", None),
            P("col", "row", None),
            P("col", "row", None, None, None),
            P(),
            P(),
            P(),
            P(("row", "col"), None),
        ),
        out_specs=(P(("row", "col"), None), P(("row", "col"), None), P(), P(), P()),
        check_vma=False,
    )
```

```python
import functools
import math

import jax
import jax.numpy as jnp
from jax import lax
from jax.experimental import pallas as pl
from jax.experimental.pallas import tpu as pltpu
from jax.sharding import PartitionSpec as P

NY, NX, NZ, NC = 4, 2, 8, 4
TILE = 128
RING = 16
bf16, f32 = jnp.bfloat16, jnp.float32


def row_id(y, x, z):
    return (y % NY * NX + x % NX) * NZ + z % NZ


def row_perm(move):
    return [
        (row_id(y, x, z), row_id(*move(y, x, z)))
        for y in range(NY)
        for x in range(NX)
        for z in range(NZ)
    ]


def shift_z(a, d):
    return lax.ppermute(a, "row", row_perm(lambda y, x, z: (y, x, z + d)))


def shift_y(a, d):
    return lax.ppermute(a, "row", row_perm(lambda y, x, z: (y + d, x, z)))


def swap_x(a):
    return lax.ppermute(a, "row", row_perm(lambda y, x, z: (y, 1 - x, z)))


def swap_bits(a, name, size, bit):
    return lax.ppermute(a, name, [(i, i ^ bit) for i in range(size)])


def swap_col(a, bit):
    return swap_bits(a, "col", NC, bit)


OFFSETS_Y = (0, -1, 1, 2)
OFFSETS_Z = (0, -1, 1, -2, 2, -3, 3, 4)


def ring_place(step, n):
    return jnp.where(step < n // 2, 2 * step, jnp.where(step == n // 2, n - 1, 2 * (n - step) - 1))


PIECES = NY + NZ


def plan_tiles(tile_count, tile_rows, tile_cols):
    r, c = lax.axis_index("row"), lax.axis_index("col")
    z, x, y = r % NZ, r // NZ % NX, r // (NZ * NX)
    count, rows, cols = tile_count[0, 0], tile_rows[0, 0], tile_cols[0, 0]
    zi = ring_place((cols % NZ - z) % NZ, NZ)
    yi = ring_place((cols // (NZ * NX) - y) % NY, NY)
    u = rows ^ c
    slots = jnp.arange(rows.shape[0], dtype=jnp.int32)
    key = jnp.where(
        cols // NZ % NX == 0, yi * 32 + u * NZ + zi, (NY + zi) * 32 + u * NY + yi
    )
    key = jnp.where(slots < count, key, PIECES * 32)
    order = key * rows.shape[0] + slots
    rank = jnp.sum((order[None, :] < order[:, None]).astype(jnp.int32), axis=1)
    listed = jnp.sum(jnp.where(rank[:, None] == slots[None, :], order[:, None], 0), axis=0)
    edges = jnp.arange(16, dtype=jnp.int32) * 32
    starts = jnp.sum((key[None, :] < edges[:, None]).astype(jnp.int32), axis=1)
    return starts, listed


def dense_kernel(pieces, starts, listed, values, after, *rest):
    outs, (total, ring, sems) = rest[:-3], rest[-3:]
    slot_count = listed.shape[0]
    first, last = starts[pieces[0]], starts[pieces[-1] + 1]

    def fetch(j):
        b = lax.rem(j, RING)
        return pltpu.make_async_copy(
            values.at[lax.rem(listed[j], slot_count)], ring.at[b], sems.at[b]
        )

    for b in range(RING):

        @pl.when(first + b < last)
        def _():
            fetch(first + b).start()

    total[...] = jnp.zeros_like(total)
    for piece, out in zip(pieces, outs):
        out[...] = jnp.zeros_like(out)
        wide = out.shape[1] // TILE

        def add(j, carry):
            cell = listed[j] // slot_count
            fetch(j).wait()
            keep = (cell == carry).astype(f32)
            value = total[...] * keep + ring[lax.rem(j, RING)].astype(f32)
            total[...] = value
            place = lax.rem(cell, 32)
            u, v = place // wide, lax.rem(place, wide)
            out[pl.ds(pl.multiple_of(u * TILE, TILE), TILE), pl.ds(pl.multiple_of(v * TILE, TILE), TILE)] = (
                value.astype(bf16)
            )

            @pl.when(j + RING < last)
            def _():
                fetch(j + RING).start()

            return cell

        lax.fori_loop(starts[piece], starts[piece + 1], add, -1)


def dense_part(pieces, starts, listed, values, after):
    shapes = [
        jax.ShapeDtypeStruct((NC * TILE, (NZ if p < NY else NY) * TILE), bf16) for p in pieces
    ]
    return pl.pallas_call(
        functools.partial(dense_kernel, pieces),
        out_shape=shapes,
        in_specs=[
            pl.BlockSpec(memory_space=pltpu.SMEM),
            pl.BlockSpec(memory_space=pltpu.SMEM),
            pl.BlockSpec(memory_space=pl.ANY),
            pl.BlockSpec(memory_space=pl.ANY),
        ],
        out_specs=[pl.BlockSpec(memory_space=pltpu.VMEM)] * len(pieces),
        scratch_shapes=[
            pltpu.VMEM((TILE, TILE), f32),
            pltpu.VMEM((RING, TILE, TILE), bf16),
            pltpu.SemaphoreType.DMA((RING,)),
        ],
        compiler_params=pltpu.CompilerParams(vmem_limit_bytes=8 * 2**20),
        cost_estimate=pl.CostEstimate(flops=4 * 10**6, bytes_accessed=10 * 2**20, transcendentals=0),
        name=f"dense{pieces[0]}",
    )(starts, listed, values, after)


def gather_direct(block, shift, offsets):
    return [block] + [shift(block, -d) for d in offsets[1:]]


def dot(a, b):
    return jnp.dot(a, b, preferred_element_type=f32)


def dot_t(a, b):
    return lax.dot_general(a, b, (((0,), (0,)), ((), ())), preferred_element_type=f32)


def add_up(parts):
    parts = [p.astype(f32) for p in parts]
    while len(parts) > 1:
        half = len(parts) // 2
        parts = [a + b for a, b in zip(parts[:half], parts[half:])]
    return parts[0]


def shards(
    features,
    degree,
    tile_count,
    tile_rows,
    tile_cols,
    tile_values,
    w_self,
    w_neigh,
    bias_term,
    grad_out,
):
    r, c = lax.axis_index("row"), lax.axis_index("col")
    x = r // NZ % NX
    nodes, width = features.shape
    node_total = nodes * NY * NX * NZ * NC

    other = swap_x(features)
    block0 = jnp.where(x == 0, features, other)
    block1 = jnp.where(x == 0, other, features)
    line_y = jnp.concatenate(gather_direct(block1, shift_y, OFFSETS_Y), axis=0)
    line_z = jnp.concatenate(gather_direct(block0, shift_z, OFFSETS_Z), axis=0)
    plane_z = [line_y]
    down = up = line_y
    for _ in range(NZ // 2 - 1):
        down, up = shift_z(down, 1), shift_z(up, -1)
        plane_z += [down, up]
    plane_z.append(shift_z(down, 1))
    half = line_z.shape[0] // 2
    down, up = shift_y(line_z, 1), shift_y(line_z, -1)
    far = jnp.concatenate([shift_y(down[:half], 1), shift_y(up[half:], -1)], axis=0)
    plane_y = [line_z, down, up, far]

    starts, listed = plan_tiles(tile_count, tile_rows, tile_cols)
    values = tile_values[0, 0]
    dense = []
    for pieces, after in (
        ((0, 1), plane_z[0]),
        ((2, 3), plane_z[1]),
        ((4, 5, 6, 7), plane_z[3]),
        ((8, 9, 10, 11), plane_z[5]),
    ):
        dense += dense_part(pieces, starts, listed, values, after)
    dense_y, dense_z = dense[:NY], dense[NY:]

    partial_sum = jnp.zeros((NC * TILE, width), f32)
    for a, b in zip(dense, plane_y + plane_z):
        partial_sum = partial_sum + dot(a, b)

    agg_sum = partial_sum[:nodes]
    for k in range(1, NC):
        sent = partial_sum[k * nodes : (k + 1) * nodes].astype(bf16)
        agg_sum = agg_sum + swap_col(sent, k).astype(f32)

    divisor = degree[:, None].astype(f32)
    aggregate = (agg_sum / divisor).astype(bf16)
    pre_act = dot(features, w_self) + dot(aggregate, w_neigh) + bias_term
    sigmoid_pre = jax.nn.sigmoid(pre_act)
    layer_out = (pre_act * sigmoid_pre).astype(bf16)
    grad_pre = (
        grad_out.astype(f32) * (sigmoid_pre * (1.0 + pre_act * (1.0 - sigmoid_pre)))
    ).astype(bf16)
    scaled_grad = (dot(grad_pre, w_neigh.T) / divisor).astype(bf16)

    row_grads = jnp.concatenate(
        [scaled_grad] + [swap_col(scaled_grad, k) for k in range(1, NC)], axis=0
    )

    norm_scale = 1.0 / math.sqrt(node_total)
    local = dot_t(jnp.concatenate([features, aggregate], axis=1), grad_pre) * norm_scale
    local_bias = jnp.sum(grad_pre.astype(f32), axis=0, keepdims=True) * norm_scale
    local_bias = jnp.pad(local_bias, ((0, 15), (0, 0))).astype(bf16)

    def share(k):
        part = lax.dynamic_slice_in_dim(local, (c ^ k) * nodes, nodes, axis=0)
        return jnp.concatenate([part.astype(bf16), local_bias], axis=0)

    rider = add_up([share(0)] + [swap_col(share(k), k) for k in range(1, NC)]).astype(bf16)

    terms_y = [dot_t(a, row_grads) for a in dense_y]
    terms_z = [dot_t(a, row_grads) for a in dense_z]

    far = terms_y[3]
    half = far.shape[0] // 2
    down, up = shift_y(far[:half].astype(bf16), 1), shift_y(far[half:].astype(bf16), -1)
    plus = jnp.concatenate([terms_y[2][:half] + down.astype(f32), terms_y[2][half:]], axis=0)
    minus = jnp.concatenate([terms_y[1][:half], terms_y[1][half:] + up.astype(f32)], axis=0)
    down, up = shift_y(plus.astype(bf16), 1), shift_y(minus.astype(bf16), -1)
    back_z = terms_y[0] + down.astype(f32) + up.astype(f32)

    size = terms_z[0].shape[0]
    riders = [rider] + [None] * (NZ - 1)
    riders[NZ // 2] = shift_z(rider, NZ // 2)
    down = shift_z(terms_z[NZ - 1].astype(bf16), 1)
    up, down_rider, up_rider = None, rider, rider
    for step in range(NZ // 2 - 1, 0, -1):
        plus, minus = terms_z[2 * step] + down.astype(f32), terms_z[2 * step - 1]
        if up is not None:
            minus = minus + up.astype(f32)
        down = shift_z(jnp.concatenate([plus.astype(bf16), down_rider], axis=0), 1)
        up = shift_z(jnp.concatenate([minus.astype(bf16), up_rider], axis=0), -1)
        down, down_rider = down[:size], down[size:]
        up, up_rider = up[:size], up[size:]
        riders[NZ // 2 + step], riders[NZ // 2 - step] = down_rider, up_rider
    back_y = terms_z[0] + down.astype(f32) + up.astype(f32)

    rider = add_up(riders).astype(bf16)
    sum1, riders = back_y[:nodes], [rider] + [None] * (NY - 1)
    for i, d in enumerate(OFFSETS_Y[1:], 1):
        block = back_y[i * nodes : (i + 1) * nodes].astype(bf16)
        got = shift_y(jnp.concatenate([block, rider], axis=0), d)
        sum1 = sum1 + got[:nodes].astype(f32)
        riders[-d % NY] = got[nodes:]
    sum0 = back_z[:nodes]
    for i, d in enumerate(OFFSETS_Z[1:], 1):
        block = back_z[i * nodes : (i + 1) * nodes].astype(bf16)
        sum0 = sum0 + shift_z(block, d).astype(f32)

    total = add_up(riders)
    total = total + swap_x(total)
    quarter = total[:nodes].astype(bf16)
    quarters = jnp.stack([quarter] + [swap_col(quarter, k) for k in range(1, NC)])
    grads = quarters[c ^ jnp.arange(NC, dtype=jnp.int32)].reshape(NC * nodes, width).astype(f32)

    kept = jnp.where(x == 0, sum0, sum1)
    sent = jnp.where(x == 0, sum1, sum0)
    neighbor_back = kept + swap_x(sent)
    grad_input = (dot(grad_pre, w_self.T) + neighbor_back).astype(bf16)
    return (layer_out, grad_input, grads[:width], grads[width:], total[nodes])


def solution(mesh):
    return jax.shard_map(
        shards,
        mesh=mesh,
        in_specs=(
            P(("row", "col"), None),
            P(("row", "col")),
            P("col", "row"),
            P("col", "row", None),
            P("col", "row", None),
            P("col", "row", None, None, None),
            P(),
            P(),
            P(),
            P(("row", "col"), None),
        ),
        out_specs=(P(("row", "col"), None), P(("row", "col"), None), P(), P(), P()),
        check_vma=False,
    )
```

```python
import functools
import math

import jax
import jax.numpy as jnp
from jax import lax
from jax.experimental import pallas as pl
from jax.experimental.pallas import tpu as pltpu
from jax.sharding import PartitionSpec as P

NY, NX, NZ, NC = 4, 2, 8, 4
TILE = 128
RING = 16
bf16, f32 = jnp.bfloat16, jnp.float32


def row_id(y, x, z):
    return (y % NY * NX + x % NX) * NZ + z % NZ


def row_perm(move):
    return [
        (row_id(y, x, z), row_id(*move(y, x, z)))
        for y in range(NY)
        for x in range(NX)
        for z in range(NZ)
    ]


def shift_z(a, d):
    return lax.ppermute(a, "row", row_perm(lambda y, x, z: (y, x, z + d)))


def shift_y(a, d):
    return lax.ppermute(a, "row", row_perm(lambda y, x, z: (y + d, x, z)))


def swap_x(a):
    return lax.ppermute(a, "row", row_perm(lambda y, x, z: (y, 1 - x, z)))


def swap_bits(a, name, size, bit):
    return lax.ppermute(a, name, [(i, i ^ bit) for i in range(size)])


def swap_col(a, bit):
    return swap_bits(a, "col", NC, bit)


OFFSETS_Y = (0, -1, 1, 2)


def ring_place(step, n):
    return jnp.where(step < n // 2, 2 * step, jnp.where(step == n // 2, n - 1, 2 * (n - step) - 1))


PIECES = NY + NZ
REPEATS = 16 * 32


def plan_tiles(tile_count, tile_rows, tile_cols):
    r, c = lax.axis_index("row"), lax.axis_index("col")
    z, x, y = r % NZ, r // NZ % NX, r // (NZ * NX)
    count, rows, cols = tile_count[0, 0], tile_rows[0, 0], tile_cols[0, 0]
    zi = ring_place((cols % NZ - z) % NZ, NZ)
    yi = ring_place((cols // (NZ * NX) - y) % NY, NY)
    u = rows ^ c
    slots = jnp.arange(rows.shape[0], dtype=jnp.int32)
    key = jnp.where(
        cols // NZ % NX == 0, yi * 32 + u * NZ + zi, (NY + zi) * 32 + u * NY + yi
    )
    live = slots < count
    same = (key[None, :] == key[:, None]) & (slots[None, :] < slots[:, None]) & live[None, :]
    repeat = jnp.any(same, axis=1)
    key = jnp.where(live, jnp.where(repeat, key + REPEATS, key), 2 * REPEATS)
    order = key * rows.shape[0] + slots
    rank = jnp.sum((order[None, :] < order[:, None]).astype(jnp.int32), axis=1)
    listed = jnp.sum(jnp.where(rank[:, None] == slots[None, :], order[:, None], 0), axis=0)
    edges = jnp.arange(32, dtype=jnp.int32) * 32
    starts = jnp.sum((key[None, :] < edges[:, None]).astype(jnp.int32), axis=1)
    return starts, listed


def dense_kernel(pieces, starts, listed, values, after, *rest):
    outs, (total, ring, sems, placed) = rest[:-4], rest[-4:]
    slot_count = listed.shape[0]
    second = REPEATS // 32
    first, last = starts[second + pieces[0]], starts[second + pieces[-1] + 1]

    def fetch(j):
        b = j & (RING - 1)
        return pltpu.make_async_copy(
            values.at[listed[j] & (slot_count - 1)], ring.at[b], sems.at[b]
        )

    for b in range(RING):

        @pl.when(first + b < last)
        def _():
            fetch(first + b).start()

    def window(out, cell):
        wide = out.shape[1] // TILE
        place = cell & 31
        u, v = place // wide, place & (wide - 1)
        return out.at[pl.ds(pl.multiple_of(u * TILE, TILE), TILE), pl.ds(pl.multiple_of(v * TILE, TILE), TILE)]

    def put(out, j):
        entry = listed[j]
        return pltpu.make_async_copy(
            values.at[entry & (slot_count - 1)], window(out, entry // slot_count), placed
        )

    for piece, out in zip(pieces, outs):

        def clear(i, carry):
            out[pl.ds(pl.multiple_of(i * 64, 64), 64), :] = jnp.zeros((64, out.shape[1]), bf16)
            return carry

        lax.fori_loop(0, out.shape[0] // 64, clear, 0)

    for piece, out in zip(pieces, outs):

        def place_first(j, carry):
            put(out, j).start()
            return carry

        lax.fori_loop(starts[piece], starts[piece + 1], place_first, 0)

    for piece, out in zip(pieces, outs):

        def wait_first(j, carry):
            put(out, j).wait()
            return carry

        lax.fori_loop(starts[piece], starts[piece + 1], wait_first, 0)

    for piece, out in zip(pieces, outs):

        def add(j, carry):
            cell = listed[j] // slot_count
            fetch(j).wait()
            spot = window(out, cell)
            base = jnp.where(cell == carry, total[...], spot[...].astype(f32))
            value = base + ring[j & (RING - 1)].astype(f32)
            total[...] = value
            spot[...] = value.astype(bf16)

            @pl.when(j + RING < last)
            def _():
                fetch(j + RING).start()

            return cell

        lax.fori_loop(starts[second + piece], starts[second + piece + 1], add, -1)


def dense_part(pieces, starts, listed, values, after):
    shapes = [
        jax.ShapeDtypeStruct((NC * TILE, (NZ if p < NY else NY) * TILE), bf16) for p in pieces
    ]
    return pl.pallas_call(
        functools.partial(dense_kernel, pieces),
        out_shape=shapes,
        in_specs=[
            pl.BlockSpec(memory_space=pltpu.SMEM),
            pl.BlockSpec(memory_space=pltpu.SMEM),
            pl.BlockSpec(memory_space=pltpu.HBM),
            pl.BlockSpec(memory_space=pl.ANY),
        ],
        out_specs=[pl.BlockSpec(memory_space=pltpu.VMEM)] * len(pieces),
        scratch_shapes=[
            pltpu.VMEM((TILE, TILE), f32),
            pltpu.VMEM((RING, TILE, TILE), bf16),
            pltpu.SemaphoreType.DMA((RING,)),
            pltpu.SemaphoreType.DMA,
        ],
        compiler_params=pltpu.CompilerParams(vmem_limit_bytes=8 * 2**20),
        cost_estimate=pl.CostEstimate(flops=4 * 10**6, bytes_accessed=10 * 2**20, transcendentals=0),
        name=f"dense{pieces[0]}",
    )(starts, listed, values, after)


def dot(a, b):
    return jnp.dot(a, b, preferred_element_type=f32)


def dot_t(a, b):
    return lax.dot_general(a, b, (((0,), (0,)), ((), ())), preferred_element_type=f32)


def add_up(parts):
    parts = [p.astype(f32) for p in parts]
    while len(parts) > 1:
        half = len(parts) // 2
        parts = [a + b for a, b in zip(parts[:half], parts[half:])]
    return parts[0]


def shards(
    features,
    degree,
    tile_count,
    tile_rows,
    tile_cols,
    tile_values,
    w_self,
    w_neigh,
    bias_term,
    grad_out,
):
    r, c = lax.axis_index("row"), lax.axis_index("col")
    x = r // NZ % NX
    nodes, width = features.shape
    node_total = nodes * NY * NX * NZ * NC

    starts, listed = plan_tiles(tile_count, tile_rows, tile_cols)
    values = tile_values[0, 0]

    other = swap_x(features)
    block0 = jnp.where(x == 0, features, other)
    block1 = jnp.where(x == 0, other, features)
    down1, up1 = shift_z(block0, 1), shift_z(block0, -1)
    line_y = jnp.concatenate(
        [block1, shift_y(block1, 1), shift_y(block1, -1), shift_y(block1, 2)], axis=0
    )
    size = line_y.shape[0]
    down2 = shift_z(jnp.concatenate([line_y, down1], axis=0), 1)
    up2 = shift_z(jnp.concatenate([line_y, up1], axis=0), -1)
    down3, up3 = shift_z(down2, 1), shift_z(up2, -1)
    far = shift_z(down2[size:], 2)
    line_z = jnp.concatenate(
        [block0, down1, up1, down2[size:], up2[size:], down3[size:], up3[size:], far], axis=0
    )
    down4, up4 = shift_z(down3[:size], 1), shift_z(up3[:size], -1)
    down5 = shift_z(down4, 1)
    plane_z = [line_y, down2[:size], up2[:size], down3[:size], up3[:size], down4, up4, down5]
    half = line_z.shape[0] // 2
    down, up = shift_y(line_z, 1), shift_y(line_z, -1)
    far = jnp.concatenate([shift_y(down[:half], 1), shift_y(up[half:], -1)], axis=0)
    plane_y = [line_z, down, up, far]

    dense_z = dense_part((4, 5, 6, 7), starts, listed, values, line_y)
    dense_z += dense_part((8, 9, 10, 11), starts, listed, values, down2)
    dense_y = dense_part((0, 1), starts, listed, values, down3)
    dense_y += dense_part((2, 3), starts, listed, values, down4)
    dense = [*dense_y, *dense_z]

    partial_sum = jnp.zeros((NC * TILE, width), f32)
    for a, b in zip(dense, plane_y + plane_z):
        partial_sum = partial_sum + dot(a, b)

    agg_sum = partial_sum[:nodes]
    for k in range(1, NC):
        sent = partial_sum[k * nodes : (k + 1) * nodes].astype(f32 if k == 1 else bf16)
        agg_sum = agg_sum + swap_col(sent, k).astype(f32)

    divisor = degree[:, None].astype(f32)
    aggregate = (agg_sum / divisor).astype(bf16)
    pre_act = dot(features, w_self) + dot(aggregate, w_neigh) + bias_term
    sigmoid_pre = jax.nn.sigmoid(pre_act)
    layer_out = (pre_act * sigmoid_pre).astype(bf16)
    grad_pre = (
        grad_out.astype(f32) * (sigmoid_pre * (1.0 + pre_act * (1.0 - sigmoid_pre)))
    ).astype(bf16)
    scaled_grad = (dot(grad_pre, w_neigh.T) / divisor).astype(bf16)

    norm_scale = 1.0 / math.sqrt(node_total)
    local = dot_t(jnp.concatenate([features, aggregate], axis=1), grad_pre) * norm_scale
    local_bias = jnp.sum(grad_pre.astype(f32), axis=0, keepdims=True) * norm_scale
    local_bias = jnp.pad(local_bias, ((0, 15), (0, 0))).astype(bf16)

    def packet(k):
        part = lax.dynamic_slice_in_dim(local, (c ^ k) * nodes, nodes, axis=0)
        return jnp.concatenate([scaled_grad, part.astype(bf16), local_bias], axis=0)

    packets = [packet(0)] + [swap_col(packet(k), k) for k in range(1, NC)]
    row_grads = jnp.concatenate([p[:nodes] for p in packets], axis=0)
    rider = add_up([p[nodes:] for p in packets])
    rider = (rider + swap_x(rider)).astype(bf16)

    terms_y = [dot_t(a, row_grads) for a in dense_y]
    terms_z = [dot_t(a, row_grads) for a in dense_z]

    def message(*blocks):
        return jnp.concatenate([block.astype(bf16) for block in blocks], axis=0)

    wide = line_z.shape[0]
    down = shift_y(message(terms_y[3][:half]), 1).astype(f32)
    up = shift_y(message(terms_y[3][half:]), -1).astype(f32)
    down = shift_y(message(terms_y[2][:half] + down, terms_y[2][half:], rider), 1)
    up = shift_y(message(terms_y[1][:half], terms_y[1][half:] + up, rider), -1)
    rider = add_up([rider, up[wide:], shift_y(rider, 2), down[wide:]]).astype(bf16)
    back_z = terms_y[0] + down[:wide].astype(f32) + up[:wide].astype(f32)
    back_z = [back_z[i * nodes : (i + 1) * nodes] for i in range(NZ)]

    ring1 = shift_z(message(terms_z[7]), 1).astype(f32)
    down2 = shift_z(message(terms_z[6] + ring1), 1).astype(f32)
    up2 = shift_z(message(terms_z[5]), -1).astype(f32)
    down3 = shift_z(message(terms_z[4] + down2, back_z[6], rider), 1)
    up3 = shift_z(message(terms_z[3] + up2, back_z[5], rider), -1)
    far = shift_z(message(back_z[7]), 2).astype(f32)
    rider4 = shift_z(rider, 4)

    def split(got):
        return got[:size].astype(f32), got[size : size + nodes].astype(f32), got[size + nodes :]

    ring_d, block_d, rider_d1 = split(down3)
    ring_u, block_u, rider_u1 = split(up3)
    down4 = shift_z(message(terms_z[2] + ring_d, back_z[4] + block_d + far, rider_d1), 1)
    up4 = shift_z(message(terms_z[1] + ring_u, back_z[3] + block_u, rider_u1), -1)
    ring_d, block_d, rider_d2 = split(down4)
    ring_u, block_u, rider_u2 = split(up4)
    back_y = terms_z[0] + ring_d + ring_u
    down5 = shift_z(message(back_z[2] + block_d, rider_d2), 1)
    up5 = shift_z(message(back_z[1] + block_u, rider_u2), -1)
    sum0 = back_z[0] + down5[:nodes].astype(f32) + up5[:nodes].astype(f32)
    rider_d3, rider_u3 = down5[nodes:], up5[nodes:]
    sum1 = back_y[:nodes]
    for i, d in enumerate(OFFSETS_Y[1:], 1):
        sum1 = sum1 + shift_y(message(back_y[i * nodes : (i + 1) * nodes]), d).astype(f32)

    total = add_up(
        [rider, rider_u1, rider_u2, rider_u3, rider4, rider_d3, rider_d2, rider_d1]
    )
    quarter = total[:nodes].astype(bf16)
    quarters = jnp.stack([quarter] + [swap_col(quarter, k) for k in range(1, NC)])
    grads = quarters[c ^ jnp.arange(NC, dtype=jnp.int32)].reshape(NC * nodes, width).astype(f32)

    kept = jnp.where(x == 0, sum0, sum1)
    sent = jnp.where(x == 0, sum1, sum0)
    neighbor_back = kept + swap_x(sent)
    grad_input = (dot(grad_pre, w_self.T) + neighbor_back).astype(bf16)
    return (layer_out, grad_input, grads[:width], grads[width:], total[nodes])


def solution(mesh):
    return jax.shard_map(
        shards,
        mesh=mesh,
        in_specs=(
            P(("row", "col"), None),
            P(("row", "col")),
            P("col", "row"),
            P("col", "row", None),
            P("col", "row", None),
            P("col", "row", None, None, None),
            P(),
            P(),
            P(),
            P(("row", "col"), None),
        ),
        out_specs=(P(("row", "col"), None), P(("row", "col"), None), P(), P(), P()),
        check_vma=False,
    )
```

```python
import functools
import math

import jax
import jax.numpy as jnp
from jax import lax
from jax.experimental import pallas as pl
from jax.experimental.pallas import tpu as pltpu
from jax.sharding import PartitionSpec as P

NY, NX, NZ, NC = 4, 2, 8, 4
TILE = 128
bf16, f32 = jnp.bfloat16, jnp.float32


def row_id(y, x, z):
    return (y % NY * NX + x % NX) * NZ + z % NZ


def row_perm(move):
    return [
        (row_id(y, x, z), row_id(*move(y, x, z)))
        for y in range(NY)
        for x in range(NX)
        for z in range(NZ)
    ]


def shift_z(a, d):
    return lax.ppermute(a, "row", row_perm(lambda y, x, z: (y, x, z + d)))


def shift_y(a, d):
    return lax.ppermute(a, "row", row_perm(lambda y, x, z: (y + d, x, z)))


def swap_x(a):
    return lax.ppermute(a, "row", row_perm(lambda y, x, z: (y, 1 - x, z)))


def swap_bits(a, name, size, bit):
    return lax.ppermute(a, name, [(i, i ^ bit) for i in range(size)])


def swap_col(a, bit):
    return swap_bits(a, "col", NC, bit)


OFFSETS_Y = (0, -1, 1, 2)


def ring_place(step, n):
    return jnp.where(step < n // 2, 2 * step, jnp.where(step == n // 2, n - 1, 2 * (n - step) - 1))


PIECES = NY + NZ
REPEATS = 16 * 32


def plan_tiles(tile_count, tile_rows, tile_cols):
    r, c = lax.axis_index("row"), lax.axis_index("col")
    z, x, y = r % NZ, r // NZ % NX, r // (NZ * NX)
    count, rows, cols = tile_count[0, 0], tile_rows[0, 0], tile_cols[0, 0]
    zi = ring_place((cols % NZ - z) % NZ, NZ)
    yi = ring_place((cols // (NZ * NX) - y) % NY, NY)
    u = rows ^ c
    slots = jnp.arange(rows.shape[0], dtype=jnp.int32)
    key = jnp.where(
        cols // NZ % NX == 0, yi * 32 + u * NZ + zi, (NY + zi) * 32 + u * NY + yi
    )
    live = slots < count
    same = (key[None, :] == key[:, None]) & (slots[None, :] < slots[:, None]) & live[None, :]
    repeat = jnp.any(same, axis=1)
    key = jnp.where(live, jnp.where(repeat, key + REPEATS, key), 2 * REPEATS)
    order = key * rows.shape[0] + slots
    rank = jnp.sum((order[None, :] < order[:, None]).astype(jnp.int32), axis=1)
    listed = jnp.sum(jnp.where(rank[:, None] == slots[None, :], order[:, None], 0), axis=0)
    edges = jnp.arange(32, dtype=jnp.int32) * 32
    starts = jnp.sum((key[None, :] < edges[:, None]).astype(jnp.int32), axis=1)
    return starts, listed


def dense_kernel(starts, listed, values, after, *rest):
    outs, total = rest[:-1], rest[-1]
    slot_count = listed.shape[0]

    def window(out, entry):
        wide = out.shape[1] // TILE
        place = (entry // slot_count) & 31
        u, v = place // wide, place & (wide - 1)
        return out.at[pl.ds(pl.multiple_of(u * TILE, TILE), TILE), pl.ds(pl.multiple_of(v * TILE, TILE), TILE)]

    for piece, out in enumerate(outs):

        def clear(i, carry):
            out[pl.ds(pl.multiple_of(i * 64, 64), 64), :] = jnp.zeros((64, out.shape[1]), bf16)
            return carry

        def place_first(j, carry):
            entry = listed[j]
            window(out, entry)[...] = values[entry & (slot_count - 1)]
            return carry

        def add(j, carry):
            entry = listed[j]
            cell = entry // slot_count
            spot = window(out, entry)
            base = jnp.where(cell == carry, total[...], spot[...].astype(f32))
            value = base + values[entry & (slot_count - 1)].astype(f32)
            total[...] = value
            spot[...] = value.astype(bf16)
            return cell

        lax.fori_loop(0, out.shape[0] // 64, clear, 0)
        lax.fori_loop(starts[piece], starts[piece + 1], place_first, 0)
        again = REPEATS // 32 + piece
        lax.fori_loop(starts[again], starts[again + 1], add, -1)


VMEM = pl.BlockSpec(memory_space=pltpu.VMEM)
SMEM = pl.BlockSpec(memory_space=pltpu.SMEM)


def dense_pieces(starts, listed, values, after):
    shapes = [
        jax.ShapeDtypeStruct((NC * TILE, (NZ if p < NY else NY) * TILE), bf16)
        for p in range(PIECES)
    ]
    return pl.pallas_call(
        dense_kernel,
        out_shape=shapes,
        in_specs=[SMEM, SMEM, VMEM, pl.BlockSpec(memory_space=pl.ANY)],
        out_specs=[VMEM] * PIECES,
        scratch_shapes=[pltpu.VMEM((TILE, TILE), f32)],
        compiler_params=pltpu.CompilerParams(vmem_limit_bytes=24 * 2**20),
        cost_estimate=pl.CostEstimate(flops=4 * 10**6, bytes_accessed=16 * 2**20, transcendentals=0),
        name="dense",
    )(starts, listed, values, after)


def last_dot_kernel(so_far, weights, near, far, *outs):
    half = near.shape[0]
    for k, out in enumerate(outs):
        rows = slice(k * TILE, (k + 1) * TILE)
        out[...] = (
            so_far[rows, :] + dot(weights[rows, :half], near[...]) + dot(weights[rows, half:], far[...])
        ).astype(out.dtype)


def last_dot(so_far, weights, near, far, types):
    shape = (TILE, so_far.shape[1])
    return pl.pallas_call(
        last_dot_kernel,
        out_shape=[jax.ShapeDtypeStruct(shape, t) for t in types],
        in_specs=[VMEM] * 4,
        out_specs=[VMEM] * len(types),
        compiler_params=pltpu.CompilerParams(vmem_limit_bytes=8 * 2**20),
        cost_estimate=pl.CostEstimate(flops=3 * 10**8, bytes_accessed=2 * 2**20, transcendentals=0),
        name="last_dot",
    )(so_far, weights, near, far)


def middle_kernel(
    scale, place, own, got1, got2, got3, self_part, features, divisor, w_neigh, grad_out,
    layer_out, grad_pre, *rest
):
    packets, local = rest[:-1], rest[-1]
    nodes, width = layer_out.shape
    agg_sum = own[...] + got1[...] + got2[...].astype(f32) + got3[...].astype(f32)
    aggregate = (agg_sum / divisor[...]).astype(bf16)
    pre_act = self_part[...] + dot(aggregate, w_neigh[...])
    sigmoid_pre = jax.nn.sigmoid(pre_act)
    layer_out[...] = (pre_act * sigmoid_pre).astype(bf16)
    grad = (
        grad_out[...].astype(f32) * (sigmoid_pre * (1.0 + pre_act * (1.0 - sigmoid_pre)))
    ).astype(bf16)
    grad_pre[...] = grad
    back = lax.dot_general(
        grad, w_neigh[...], (((1,), (1,)), ((), ())), preferred_element_type=f32
    )
    scaled = (back / divisor[...]).astype(bf16)
    local[:width, :] = (dot_t(features[...], grad) * scale).astype(bf16)
    local[width:, :] = (dot_t(aggregate, grad) * scale).astype(bf16)
    bias = jnp.sum(grad.astype(f32), axis=0, keepdims=True) * scale
    bias = jnp.where(lax.broadcasted_iota(jnp.int32, (16, width), 0) == 0, bias, 0.0).astype(bf16)
    for k, packet in enumerate(packets):
        packet[:nodes, :] = scaled
        start = pl.multiple_of((place[0] ^ k) * nodes, nodes)
        packet[nodes : 2 * nodes, :] = local[pl.ds(start, nodes), :]
        packet[2 * nodes :, :] = bias


def middle(scale, place, sums, self_part, features, divisor, w_neigh, grad_out):
    nodes, width = features.shape
    node_shape = jax.ShapeDtypeStruct((nodes, width), bf16)
    packet_shape = jax.ShapeDtypeStruct((2 * nodes + 16, width), bf16)

    def body(*refs):
        middle_kernel(scale, *refs)

    return pl.pallas_call(
        body,
        out_shape=[node_shape] * 2 + [packet_shape] * NC,
        in_specs=[SMEM] + [VMEM] * 9,
        out_specs=[VMEM] * (2 + NC),
        scratch_shapes=[pltpu.VMEM((2 * width, width), bf16)],
        compiler_params=pltpu.CompilerParams(vmem_limit_bytes=8 * 2**20),
        cost_estimate=pl.CostEstimate(flops=10**8, bytes_accessed=2 * 2**20, transcendentals=nodes * width),
        name="middle",
    )(place, *sums, self_part, features, divisor, w_neigh, grad_out)


def dot(a, b):
    return jnp.dot(a, b, preferred_element_type=f32)


def dot_t(a, b):
    return lax.dot_general(a, b, (((0,), (0,)), ((), ())), preferred_element_type=f32)


def add_up(parts):
    parts = [p.astype(f32) for p in parts]
    while len(parts) > 1:
        half = len(parts) // 2
        parts = [a + b for a, b in zip(parts[:half], parts[half:])]
    return parts[0]


def shards(
    features,
    degree,
    tile_count,
    tile_rows,
    tile_cols,
    tile_values,
    w_self,
    w_neigh,
    bias_term,
    grad_out,
):
    r, c = lax.axis_index("row"), lax.axis_index("col")
    x = r // NZ % NX
    nodes, width = features.shape
    node_total = nodes * NY * NX * NZ * NC

    starts, listed = plan_tiles(tile_count, tile_rows, tile_cols)
    values = tile_values[0, 0]

    other = swap_x(features)
    block0 = jnp.where(x == 0, features, other)
    block1 = jnp.where(x == 0, other, features)
    down1, up1 = shift_z(block0, 1), shift_z(block0, -1)
    line_y = jnp.concatenate(
        [block1, shift_y(block1, 1), shift_y(block1, -1), shift_y(block1, 2)], axis=0
    )
    size = line_y.shape[0]
    down2 = shift_z(jnp.concatenate([line_y, down1], axis=0), 1)
    up2 = shift_z(jnp.concatenate([line_y, up1], axis=0), -1)
    down3, up3 = shift_z(down2, 1), shift_z(up2, -1)
    far = shift_z(down2[size:], 2)
    line_z = jnp.concatenate(
        [block0, down1, up1, down2[size:], up2[size:], down3[size:], up3[size:], far], axis=0
    )
    down4, up4 = shift_z(down3[:size], 1), shift_z(up3[:size], -1)
    down5 = shift_z(down4, 1)
    plane_z = [line_y, down2[:size], up2[:size], down3[:size], up3[:size], down4, up4, down5]
    half = line_z.shape[0] // 2
    down, up = shift_y(line_z, 1), shift_y(line_z, -1)
    far = shift_y(down[:half], 1), shift_y(up[half:], -1)
    plane_y = [line_z, down, up]

    dense = dense_pieces(starts, listed, values, down2)
    dense_y, dense_z = dense[:NY], dense[NY:]

    so_far = None
    for a, b in zip(dense_y[:3] + dense_z, plane_y + plane_z):
        so_far = dot(a, b) if so_far is None else so_far + dot(a, b)
    sums = last_dot(so_far, dense_y[3], *far, [f32, f32, bf16, bf16])
    sums = [sums[0]] + [swap_col(sums[k], k) for k in range(1, NC)]

    divisor = degree[:, None].astype(f32)
    self_part = dot(features, w_self) + bias_term
    layer_out, grad_pre, *packets = middle(
        1.0 / math.sqrt(node_total),
        jnp.reshape(c, (1,)),
        sums,
        self_part,
        features,
        divisor,
        w_neigh,
        grad_out,
    )
    packets = [packets[0]] + [swap_col(packets[k], k) for k in range(1, NC)]
    row_grads = jnp.concatenate([p[:nodes] for p in packets], axis=0)
    rider = add_up([p[nodes:] for p in packets]).astype(bf16)

    terms_y = [dot_t(a, row_grads) for a in dense_y]
    terms_z = [dot_t(a, row_grads) for a in dense_z]

    def message(*blocks):
        return jnp.concatenate([block.astype(bf16) for block in blocks], axis=0)

    down = shift_y(message(terms_y[3][:half], rider), 1)
    up = shift_y(message(terms_y[3][half:], rider), -1)
    rider = add_up([rider, up[half:], shift_y(rider, 2), down[half:]])
    rider = (rider + swap_x(rider)).astype(bf16)
    down, up = down[:half].astype(f32), up[:half].astype(f32)
    down = shift_y(message(terms_y[2][:half] + down, terms_y[2][half:]), 1)
    up = shift_y(message(terms_y[1][:half], terms_y[1][half:] + up), -1)
    back_z = terms_y[0] + down.astype(f32) + up.astype(f32)
    back_z = [back_z[i * nodes : (i + 1) * nodes] for i in range(NZ)]

    ring1 = shift_z(message(terms_z[7]), 1).astype(f32)
    down2 = shift_z(message(terms_z[6] + ring1), 1).astype(f32)
    up2 = shift_z(message(terms_z[5]), -1).astype(f32)
    down3 = shift_z(message(terms_z[4] + down2, back_z[6], rider), 1)
    up3 = shift_z(message(terms_z[3] + up2, back_z[5], rider), -1)
    far = shift_z(message(back_z[7]), 2).astype(f32)

    down3, up3 = lax.optimization_barrier((down3, up3))

    def split(got):
        return got[:size].astype(f32), got[size : size + nodes].astype(f32), got[size + nodes :]

    ring_d, block_d, rider_d1 = split(down3)
    ring_u, block_u, rider_u1 = split(up3)
    down4 = shift_z(message(terms_z[2] + ring_d, back_z[4] + block_d + far, rider_d1), 1)
    up4 = shift_z(message(terms_z[1] + ring_u, back_z[3] + block_u, rider_u1), -1)
    down4, up4 = lax.optimization_barrier((down4, up4))
    ring_d, block_d, rider_d2 = split(down4)
    ring_u, block_u, rider_u2 = split(up4)
    rider4 = shift_z(rider_d2, 2)
    back_y = terms_z[0] + ring_d + ring_u
    down5 = shift_z(message(back_z[2] + block_d, rider_d2), 1)
    up5 = shift_z(message(back_z[1] + block_u, rider_u2), -1)
    sum0 = back_z[0] + down5[:nodes].astype(f32) + up5[:nodes].astype(f32)
    rider_d3, rider_u3 = down5[nodes:], up5[nodes:]
    sum1 = back_y[:nodes]
    for i, d in enumerate(OFFSETS_Y[1:], 1):
        sum1 = sum1 + shift_y(message(back_y[i * nodes : (i + 1) * nodes]), d).astype(f32)

    total = add_up(
        [rider, rider_u1, rider_u2, rider_u3, rider4, rider_d3, rider_d2, rider_d1]
    )
    quarter = total[:nodes].astype(bf16)
    quarters = jnp.stack([quarter] + [swap_col(quarter, k) for k in range(1, NC)])
    grads = quarters[c ^ jnp.arange(NC, dtype=jnp.int32)].reshape(NC * nodes, width).astype(f32)

    kept = jnp.where(x == 0, sum0, sum1)
    sent = jnp.where(x == 0, sum1, sum0)
    neighbor_back = kept + swap_x(sent)
    grad_input = (dot(grad_pre, w_self.T) + neighbor_back).astype(bf16)
    return (layer_out, grad_input, grads[:width], grads[width:], total[nodes])


def solution(mesh):
    return jax.shard_map(
        shards,
        mesh=mesh,
        in_specs=(
            P(("row", "col"), None),
            P(("row", "col")),
            P("col", "row"),
            P("col", "row", None),
            P("col", "row", None),
            P("col", "row", None, None, None),
            P(),
            P(),
            P(),
            P(("row", "col"), None),
        ),
        out_specs=(P(("row", "col"), None), P(("row", "col"), None), P(), P(), P()),
        check_vma=False,
    )
```

```python
import functools
import math

import jax
import jax.numpy as jnp
from jax import lax
from jax.experimental import pallas as pl
from jax.experimental.pallas import tpu as pltpu
from jax.sharding import PartitionSpec as P

NY, NX, NZ, NC = 4, 2, 8, 4
TILE = 128
bf16, f32 = jnp.bfloat16, jnp.float32


def row_id(y, x, z):
    return (y % NY * NX + x % NX) * NZ + z % NZ


def row_perm(move):
    return [
        (row_id(y, x, z), row_id(*move(y, x, z)))
        for y in range(NY)
        for x in range(NX)
        for z in range(NZ)
    ]


def shift_z(a, d):
    return lax.ppermute(a, "row", row_perm(lambda y, x, z: (y, x, z + d)))


def shift_y(a, d):
    return lax.ppermute(a, "row", row_perm(lambda y, x, z: (y + d, x, z)))


def swap_x(a):
    return lax.ppermute(a, "row", row_perm(lambda y, x, z: (y, 1 - x, z)))


def swap_bits(a, name, size, bit):
    return lax.ppermute(a, name, [(i, i ^ bit) for i in range(size)])


def swap_col(a, bit):
    return swap_bits(a, "col", NC, bit)


def ring_place(step, n):
    return jnp.where(step < n // 2, 2 * step, jnp.where(step == n // 2, n - 1, 2 * (n - step) - 1))


STRIPS = NZ // 2
PIECES = NY * STRIPS
CELLS = NC * 4
REPEATS = PIECES * CELLS


def plan_tiles(tile_count, tile_rows, tile_cols):
    r, c = lax.axis_index("row"), lax.axis_index("col")
    z, x, y = r % NZ, r // NZ % NX, r // (NZ * NX)
    count, rows, cols = tile_count[0, 0], tile_rows[0, 0], tile_cols[0, 0]
    zi = ring_place((cols % NZ - z) % NZ, NZ)
    yi = ring_place((cols // (NZ * NX) - y) % NY, NY)
    u = rows ^ c
    slots = jnp.arange(rows.shape[0], dtype=jnp.int32)
    piece = yi * STRIPS + zi // 2
    key = piece * CELLS + u * 4 + zi % 2 * 2 + (cols // NZ % NX ^ x)
    live = slots < count
    same = (key[None, :] == key[:, None]) & (slots[None, :] < slots[:, None]) & live[None, :]
    repeat = jnp.any(same, axis=1)
    key = jnp.where(live, jnp.where(repeat, key + REPEATS, key), 2 * REPEATS)
    order = key * rows.shape[0] + slots
    rank = jnp.sum((order[None, :] < order[:, None]).astype(jnp.int32), axis=1)
    listed = jnp.sum(jnp.where(rank[:, None] == slots[None, :], order[:, None], 0), axis=0)
    edges = jnp.arange(2 * PIECES + 1, dtype=jnp.int32) * CELLS
    starts = jnp.sum((key[None, :] < edges[:, None]).astype(jnp.int32), axis=1)
    return starts, listed


def dense_kernel(starts, listed, values, after, *rest):
    outs, total = rest[:-1], rest[-1]
    slot_count = listed.shape[0]

    def window(out, entry):
        place = (entry // slot_count) & (CELLS - 1)
        u, v = place // 4, place & 3
        return out.at[pl.ds(pl.multiple_of(u * TILE, TILE), TILE), pl.ds(pl.multiple_of(v * TILE, TILE), TILE)]

    for piece, out in enumerate(outs):

        def clear(i, carry):
            out[pl.ds(pl.multiple_of(i * 64, 64), 64), :] = jnp.zeros((64, out.shape[1]), bf16)
            return carry

        def place_first(j, carry):
            entry = listed[j]
            window(out, entry)[...] = values[entry & (slot_count - 1)]
            return carry

        def add(j, carry):
            entry = listed[j]
            cell = entry // slot_count
            spot = window(out, entry)
            base = jnp.where(cell == carry, total[...], spot[...].astype(f32))
            value = base + values[entry & (slot_count - 1)].astype(f32)
            total[...] = value
            spot[...] = value.astype(bf16)
            return cell

        lax.fori_loop(0, out.shape[0] // 64, clear, 0)
        lax.fori_loop(starts[piece], starts[piece + 1], place_first, 0)
        again = PIECES + piece
        lax.fori_loop(starts[again], starts[again + 1], add, -1)


VMEM = pl.BlockSpec(memory_space=pltpu.VMEM)
SMEM = pl.BlockSpec(memory_space=pltpu.SMEM)


def dense_pieces(starts, listed, values, after):
    shapes = [jax.ShapeDtypeStruct((NC * TILE, 4 * TILE), bf16)] * PIECES
    return pl.pallas_call(
        dense_kernel,
        out_shape=shapes,
        in_specs=[SMEM, SMEM, VMEM, pl.BlockSpec(memory_space=pl.ANY)],
        out_specs=[VMEM] * PIECES,
        scratch_shapes=[pltpu.VMEM((TILE, TILE), f32)],
        compiler_params=pltpu.CompilerParams(vmem_limit_bytes=4 * 2**20),
        cost_estimate=pl.CostEstimate(flops=4 * 10**6, bytes_accessed=16 * 2**20, transcendentals=0),
        name="dense",
    )(starts, listed, values, after)


def last_dot_kernel(so_far, weights0, weights1, block0, block1, *outs):
    for k, out in enumerate(outs):
        rows = slice(k * TILE, (k + 1) * TILE)
        out[...] = (
            so_far[rows, :] + dot(weights0[rows, :], block0[...]) + dot(weights1[rows, :], block1[...])
        ).astype(out.dtype)


def last_dot(so_far, weights, blocks, types):
    shape = (TILE, so_far.shape[1])
    return pl.pallas_call(
        last_dot_kernel,
        out_shape=[jax.ShapeDtypeStruct(shape, t) for t in types],
        compiler_params=pltpu.CompilerParams(vmem_limit_bytes=8 * 2**20),
        cost_estimate=pl.CostEstimate(flops=3 * 10**8, bytes_accessed=2 * 2**20, transcendentals=0),
        name="last_dot",
    )(so_far, *weights, *blocks)


def middle_kernel(
    scale, place, own, got1, got2, got3, self_part, features, divisor, w_neigh, grad_out,
    layer_out, grad_pre, *rest
):
    packets, local = rest[:-1], rest[-1]
    nodes, width = layer_out.shape
    agg_sum = own[...] + got1[...] + got2[...].astype(f32) + got3[...].astype(f32)
    aggregate = (agg_sum / divisor[...]).astype(bf16)
    pre_act = self_part[...] + dot(aggregate, w_neigh[...])
    sigmoid_pre = jax.nn.sigmoid(pre_act)
    layer_out[...] = (pre_act * sigmoid_pre).astype(bf16)
    grad = (
        grad_out[...].astype(f32) * (sigmoid_pre * (1.0 + pre_act * (1.0 - sigmoid_pre)))
    ).astype(bf16)
    grad_pre[...] = grad
    back = lax.dot_general(
        grad, w_neigh[...], (((1,), (1,)), ((), ())), preferred_element_type=f32
    )
    scaled = (back / divisor[...]).astype(bf16)
    local[:width, :] = (dot_t(features[...], grad) * scale).astype(bf16)
    local[width:, :] = (dot_t(aggregate, grad) * scale).astype(bf16)
    bias = jnp.sum(grad.astype(f32), axis=0, keepdims=True) * scale
    bias = jnp.where(lax.broadcasted_iota(jnp.int32, (16, width), 0) == 0, bias, 0.0).astype(bf16)
    for k, packet in enumerate(packets):
        packet[:nodes, :] = scaled
        start = pl.multiple_of((place[0] ^ k) * nodes, nodes)
        packet[nodes : 2 * nodes, :] = local[pl.ds(start, nodes), :]
        packet[2 * nodes :, :] = bias


def middle(scale, place, sums, self_part, features, divisor, w_neigh, grad_out):
    nodes, width = features.shape
    node_shape = jax.ShapeDtypeStruct((nodes, width), bf16)
    packet_shape = jax.ShapeDtypeStruct((2 * nodes + 16, width), bf16)

    def body(*refs):
        middle_kernel(scale, *refs)

    return pl.pallas_call(
        body,
        out_shape=[node_shape] * 2 + [packet_shape] * NC,
        in_specs=[SMEM] + [pl.BlockSpec()] * 9,
        scratch_shapes=[pltpu.VMEM((2 * width, width), bf16)],
        compiler_params=pltpu.CompilerParams(vmem_limit_bytes=8 * 2**20),
        cost_estimate=pl.CostEstimate(flops=10**8, bytes_accessed=2 * 2**20, transcendentals=nodes * width),
        name="middle",
    )(place, *sums, self_part, features, divisor, w_neigh, grad_out)


def dot(a, b):
    return jnp.dot(a, b, preferred_element_type=f32)


def dot_t(a, b):
    return lax.dot_general(a, b, (((0,), (0,)), ((), ())), preferred_element_type=f32)


def add_up(parts):
    parts = [p.astype(f32) for p in parts]
    while len(parts) > 1:
        half = len(parts) // 2
        parts = [a + b for a, b in zip(parts[:half], parts[half:])]
    return parts[0]


def shards(
    features,
    degree,
    tile_count,
    tile_rows,
    tile_cols,
    tile_values,
    w_self,
    w_neigh,
    bias_term,
    grad_out,
):
    c = lax.axis_index("col")
    nodes, width = features.shape
    node_total = nodes * NY * NX * NZ * NC

    starts, listed = plan_tiles(tile_count, tile_rows, tile_cols)
    values = tile_values[0, 0]

    pair = jnp.concatenate([features, swap_x(features)], axis=0)
    down = up = pair
    line = [pair]
    for _ in range(NZ // 2 - 1):
        down, up = shift_z(down, 1), shift_z(up, -1)
        line += [down, up]
    line.append(shift_z(down, 1))
    strips = [jnp.concatenate(line[2 * p : 2 * p + 2], axis=0) for p in range(STRIPS)]
    downs = [shift_y(strip, 1) for strip in strips]
    ups = [shift_y(strip, -1) for strip in strips]
    fars = [shift_y(ups[p], -1) if p % 2 else shift_y(downs[p], 1) for p in range(STRIPS)]
    blocks = strips + downs + ups + fars

    dense = dense_pieces(starts, listed, values, line[3])

    so_far = None
    for a, b in zip(dense[:-2], blocks[:-2]):
        so_far = dot(a, b) if so_far is None else so_far + dot(a, b)
    sums = last_dot(so_far, dense[-2:], blocks[-2:], [f32, f32, bf16, bf16])
    sums = [sums[0]] + [swap_col(sums[k], k) for k in range(1, NC)]

    divisor = degree[:, None].astype(f32)
    self_part = dot(features, w_self) + bias_term
    layer_out, grad_pre, *packets = middle(
        1.0 / math.sqrt(node_total),
        jnp.reshape(c, (1,)),
        sums,
        self_part,
        features,
        divisor,
        w_neigh,
        grad_out,
    )
    packets = [packets[0]] + [swap_col(packets[k], k) for k in range(1, NC)]
    row_grads = jnp.concatenate([p[:nodes] for p in packets], axis=0)
    rider = add_up([p[nodes:] for p in packets]).astype(bf16)

    terms = [dot_t(a, row_grads) for a in dense]
    wide = terms[0].shape[0]

    def message(*blocks):
        return jnp.concatenate([block.astype(bf16) for block in blocks], axis=0)

    def along_y(p, riding):
        mine, before, after, far = (terms[i * STRIPS + p] for i in range(NY))
        if p % 2:
            first = shift_y(message(far, *riding), -1)
            down = shift_y(message(after, *riding), 1)
            passed = [first[wide:]] if riding else []
            up = shift_y(message(before + first[:wide].astype(f32), *passed), -1)
        else:
            first = shift_y(message(far), 1)
            up = shift_y(message(before), -1)
            down = shift_y(message(after + first.astype(f32)), 1)
        total = mine + down[:wide].astype(f32) + up[:wide].astype(f32)
        got = [first[wide:], up[wide:], down[wide:]] if riding else []
        return [total[: wide // 2], total[wide // 2 :]], got

    (plus3, far), got = along_y(3, [rider])
    rider = add_up([rider, *got])
    rider = (rider + swap_x(rider)).astype(bf16)
    (plus2, minus3), _ = along_y(2, [])
    (plus1, minus2), _ = along_y(1, [])
    (mine, minus1), _ = along_y(0, [])
    wide = wide // 2

    def along_z(block, riding, d):
        got = shift_z(message(block, riding), d)
        return got[:wide].astype(f32), got[wide:]

    down, down1 = along_z(far, rider, 1)
    down, down2 = along_z(plus3 + down, down1, 1)
    up, up1 = along_z(minus3, rider, -1)
    down, down3 = along_z(plus2 + down, down2, 1)
    up, up2 = along_z(minus2 + up, up1, -1)
    down, down4 = along_z(plus1 + down, down3, 1)
    up, up3 = along_z(minus1 + up, up2, -1)
    mine = mine + down + up
    total = add_up([rider, up1, up2, up3, down4, down3, down2, down1])
    quarter = total[:nodes].astype(bf16)
    quarters = jnp.stack([quarter] + [swap_col(quarter, k) for k in range(1, NC)])
    grads = quarters[c ^ jnp.arange(NC, dtype=jnp.int32)].reshape(NC * nodes, width).astype(f32)

    neighbor_back = mine[:nodes] + swap_x(mine[nodes:])
    grad_input = (dot(grad_pre, w_self.T) + neighbor_back).astype(bf16)
    return (layer_out, grad_input, grads[:width], grads[width:], total[nodes])


def solution(mesh):
    return jax.shard_map(
        shards,
        mesh=mesh,
        in_specs=(
            P(("row", "col"), None),
            P(("row", "col")),
            P("col", "row"),
            P("col", "row", None),
            P("col", "row", None),
            P("col", "row", None, None, None),
            P(),
            P(),
            P(),
            P(("row", "col"), None),
        ),
        out_specs=(P(("row", "col"), None), P(("row", "col"), None), P(), P(), P()),
        check_vma=False,
    )
```

```python
import functools
import math

import jax
import jax.numpy as jnp
from jax import lax
from jax.experimental import pallas as pl
from jax.experimental.pallas import tpu as pltpu
from jax.sharding import PartitionSpec as P

NY, NX, NZ, NC = 4, 2, 8, 4
TILE = 128
bf16, f32 = jnp.bfloat16, jnp.float32


def row_id(y, x, z):
    return (y % NY * NX + x % NX) * NZ + z % NZ


def row_perm(move):
    return [
        (row_id(y, x, z), row_id(*move(y, x, z)))
        for y in range(NY)
        for x in range(NX)
        for z in range(NZ)
    ]


def shift_z(a, d):
    return lax.ppermute(a, "row", row_perm(lambda y, x, z: (y, x, z + d)))


def shift_y(a, d):
    return lax.ppermute(a, "row", row_perm(lambda y, x, z: (y + d, x, z)))


def swap_x(a):
    return lax.ppermute(a, "row", row_perm(lambda y, x, z: (y, 1 - x, z)))


def swap_bits(a, name, size, bit):
    return lax.ppermute(a, name, [(i, i ^ bit) for i in range(size)])


def swap_col(a, bit):
    return swap_bits(a, "col", NC, bit)


OFFSETS_Y = (0, -1, 1, 2)


def ring_place(step, n):
    return jnp.where(step < n // 2, 2 * step, jnp.where(step == n // 2, n - 1, 2 * (n - step) - 1))


PIECES = NY + NZ
REPEATS = 16 * 32


def plan_tiles(tile_count, tile_rows, tile_cols):
    r, c = lax.axis_index("row"), lax.axis_index("col")
    z, x, y = r % NZ, r // NZ % NX, r // (NZ * NX)
    count, rows, cols = tile_count[0, 0], tile_rows[0, 0], tile_cols[0, 0]
    zi = ring_place((cols % NZ - z) % NZ, NZ)
    yi = ring_place((cols // (NZ * NX) - y) % NY, NY)
    u = rows ^ c
    slots = jnp.arange(rows.shape[0], dtype=jnp.int32)
    key = jnp.where(
        cols // NZ % NX == 0, yi * 32 + u * NZ + zi, (NY + zi) * 32 + u * NY + yi
    )
    live = slots < count
    same = (key[None, :] == key[:, None]) & (slots[None, :] < slots[:, None]) & live[None, :]
    repeat = jnp.any(same, axis=1)
    key = jnp.where(live, jnp.where(repeat, key + REPEATS, key), 2 * REPEATS)
    order = key * rows.shape[0] + slots
    rank = jnp.sum((order[None, :] < order[:, None]).astype(jnp.int32), axis=1)
    listed = jnp.sum(jnp.where(rank[:, None] == slots[None, :], order[:, None], 0), axis=0)
    edges = jnp.arange(32, dtype=jnp.int32) * 32
    starts = jnp.sum((key[None, :] < edges[:, None]).astype(jnp.int32), axis=1)
    return starts, listed


def dense_kernel(starts, listed, values, after, *rest):
    outs, total = rest[:-1], rest[-1]
    slot_count = listed.shape[0]

    def window(out, entry):
        wide = out.shape[1] // TILE
        place = (entry // slot_count) & 31
        u, v = place // wide, place & (wide - 1)
        return out.at[pl.ds(pl.multiple_of(u * TILE, TILE), TILE), pl.ds(pl.multiple_of(v * TILE, TILE), TILE)]

    for piece, out in enumerate(outs):

        def clear(i, carry):
            out[pl.ds(pl.multiple_of(i * 64, 64), 64), :] = jnp.zeros((64, out.shape[1]), bf16)
            return carry

        def place_first(j, carry):
            entry = listed[j]
            window(out, entry)[...] = values[entry & (slot_count - 1)]
            return carry

        def add(j, carry):
            entry = listed[j]
            cell = entry // slot_count
            spot = window(out, entry)
            base = jnp.where(cell == carry, total[...], spot[...].astype(f32))
            value = base + values[entry & (slot_count - 1)].astype(f32)
            total[...] = value
            spot[...] = value.astype(bf16)
            return cell

        lax.fori_loop(0, out.shape[0] // 64, clear, 0)
        lax.fori_loop(starts[piece], starts[piece + 1], place_first, 0)
        again = REPEATS // 32 + piece
        lax.fori_loop(starts[again], starts[again + 1], add, -1)


VMEM = pl.BlockSpec(memory_space=pltpu.VMEM)
SMEM = pl.BlockSpec(memory_space=pltpu.SMEM)


def dense_pieces(starts, listed, values, after):
    shapes = [
        jax.ShapeDtypeStruct((NC * TILE, (NZ if p < NY else NY) * TILE), bf16)
        for p in range(PIECES)
    ]
    return pl.pallas_call(
        dense_kernel,
        out_shape=shapes,
        in_specs=[SMEM, SMEM, VMEM, pl.BlockSpec(memory_space=pl.ANY)],
        out_specs=[VMEM] * PIECES,
        scratch_shapes=[pltpu.VMEM((TILE, TILE), f32)],
        compiler_params=pltpu.CompilerParams(vmem_limit_bytes=4 * 2**20),
        cost_estimate=pl.CostEstimate(flops=4 * 10**6, bytes_accessed=16 * 2**20, transcendentals=0),
        name="dense",
    )(starts, listed, values, after)


def last_dot_kernel(so_far, weights, near, far, *outs):
    half = near.shape[0]
    for k, out in enumerate(outs, 1):
        rows = slice(k * TILE, (k + 1) * TILE)
        out[...] = (
            so_far[rows, :] + dot(weights[rows, :half], near[...]) + dot(weights[rows, half:], far[...])
        ).astype(out.dtype)


def last_dot(so_far, weights, near, far, types):
    shape = (TILE, so_far.shape[1])
    return pl.pallas_call(
        last_dot_kernel,
        out_shape=[jax.ShapeDtypeStruct(shape, t) for t in types],
        in_specs=[VMEM] * 4,
        out_specs=[VMEM] * len(types),
        compiler_params=pltpu.CompilerParams(vmem_limit_bytes=8 * 2**20),
        cost_estimate=pl.CostEstimate(flops=3 * 10**8, bytes_accessed=2 * 2**20, transcendentals=0),
        name="last_dot",
    )(so_far, weights, near, far)


def middle_kernel(scale, place, divisor, *rest):
    inputs, (layer_out, grad_pre), rest = rest[:8], rest[8:10], rest[10:]
    packets, held, (local, layer_held, sems) = rest[:NC], rest[NC : NC + 8], rest[NC + 8 :]
    copies = [
        pltpu.make_async_copy(source, target, sems.at[i])
        for i, (source, target) in enumerate(zip(inputs, held))
    ]
    for copy in copies:
        copy.start()
    for copy in copies:
        copy.wait()
    own, got1, got2, got3, self_part, features, w_neigh, grad_out = held
    nodes, width = features.shape
    agg_sum = own[...] + got1[...] + got2[...].astype(f32) + got3[...].astype(f32)
    aggregate = (agg_sum / divisor[...]).astype(bf16)
    pre_act = self_part[...] + dot(aggregate, w_neigh[...])
    sigmoid_pre = jax.nn.sigmoid(pre_act)
    layer_held[...] = (pre_act * sigmoid_pre).astype(bf16)
    leave = pltpu.make_async_copy(layer_held, layer_out, sems.at[8])
    leave.start()
    grad = (
        grad_out[...].astype(f32) * (sigmoid_pre * (1.0 + pre_act * (1.0 - sigmoid_pre)))
    ).astype(bf16)
    grad_pre[...] = grad
    back = lax.dot_general(
        grad, w_neigh[...], (((1,), (1,)), ((), ())), preferred_element_type=f32
    )
    scaled = (back / divisor[...]).astype(bf16)
    local[:width, :] = (dot_t(features[...], grad) * scale).astype(bf16)
    local[width:, :] = (dot_t(aggregate, grad) * scale).astype(bf16)
    bias = jnp.sum(grad.astype(f32), axis=0, keepdims=True) * scale
    bias = jnp.where(lax.broadcasted_iota(jnp.int32, (16, width), 0) == 0, bias, 0.0).astype(bf16)
    for k, packet in enumerate(packets):
        packet[:nodes, :] = scaled
        start = pl.multiple_of((place[0] ^ k) * nodes, nodes)
        packet[nodes : 2 * nodes, :] = local[pl.ds(start, nodes), :]
        packet[2 * nodes :, :] = bias
    leave.wait()


def middle(scale, place, divisor, sums, self_part, features, w_neigh, grad_out):
    nodes, width = features.shape
    inputs = [*sums, self_part, features, w_neigh, grad_out]
    node_shape = jax.ShapeDtypeStruct((nodes, width), bf16)
    packet_shape = jax.ShapeDtypeStruct((2 * nodes + 16, width), bf16)
    anywhere = pl.BlockSpec(memory_space=pl.ANY)
    return pl.pallas_call(
        functools.partial(middle_kernel, scale),
        out_shape=[node_shape] * 2 + [packet_shape] * NC,
        in_specs=[SMEM, VMEM] + [anywhere] * 8,
        out_specs=[anywhere, VMEM] + [VMEM] * NC,
        scratch_shapes=[pltpu.VMEM(a.shape, a.dtype) for a in inputs]
        + [
            pltpu.VMEM((2 * width, width), bf16),
            pltpu.VMEM((nodes, width), bf16),
            pltpu.SemaphoreType.DMA((9,)),
        ],
        compiler_params=pltpu.CompilerParams(vmem_limit_bytes=8 * 2**20),
        cost_estimate=pl.CostEstimate(flops=10**8, bytes_accessed=2 * 2**20, transcendentals=nodes * width),
        name="middle",
    )(place, divisor, *inputs)


def dot(a, b):
    return jnp.dot(a, b, preferred_element_type=f32)


def dot_t(a, b):
    return lax.dot_general(a, b, (((0,), (0,)), ((), ())), preferred_element_type=f32)


def add_up(parts):
    parts = [p.astype(f32) for p in parts]
    while len(parts) > 1:
        half = len(parts) // 2
        parts = [a + b for a, b in zip(parts[:half], parts[half:])]
    return parts[0]


def shards(
    features,
    degree,
    tile_count,
    tile_rows,
    tile_cols,
    tile_values,
    w_self,
    w_neigh,
    bias_term,
    grad_out,
):
    r, c = lax.axis_index("row"), lax.axis_index("col")
    x = r // NZ % NX
    nodes, width = features.shape
    node_total = nodes * NY * NX * NZ * NC

    starts, listed = plan_tiles(tile_count, tile_rows, tile_cols)
    values = tile_values[0, 0]

    other = swap_x(features)
    block0 = jnp.where(x == 0, features, other)
    block1 = jnp.where(x == 0, other, features)
    down1, up1 = shift_z(block0, 1), shift_z(block0, -1)
    line_y = jnp.concatenate(
        [block1, shift_y(block1, 1), shift_y(block1, -1), shift_y(block1, 2)], axis=0
    )
    size = line_y.shape[0]
    down2 = shift_z(jnp.concatenate([line_y, down1], axis=0), 1)
    up2 = shift_z(jnp.concatenate([line_y, up1], axis=0), -1)
    down3, up3 = shift_z(down2, 1), shift_z(up2, -1)
    far = shift_z(down2[size:], 2)
    line_z = jnp.concatenate(
        [block0, down1, up1, down2[size:], up2[size:], down3[size:], up3[size:], far], axis=0
    )
    down4, up4 = shift_z(down3[:size], 1), shift_z(up3[:size], -1)
    down5 = shift_z(down4, 1)
    plane_z = [line_y, down2[:size], up2[:size], down3[:size], up3[:size], down4, up4, down5]
    half = line_z.shape[0] // 2
    down, up = shift_y(line_z, 1), shift_y(line_z, -1)
    far = shift_y(down[:half], 1), shift_y(up[half:], -1)
    plane_y = [line_z, down, up]

    dense = dense_pieces(starts, listed, values, line_z)
    dense_y, dense_z = dense[:NY], dense[NY:]

    so_far = None
    for a, b in zip(dense_y[:3] + dense_z, plane_y + plane_z):
        so_far = dot(a, b) if so_far is None else so_far + dot(a, b)
    sent = last_dot(so_far, dense_y[3], *far, [f32, bf16, bf16])
    sums = [swap_col(block, k) for k, block in enumerate(sent, 1)]
    own = so_far[:nodes] + dot(dense_y[3][:nodes], jnp.concatenate(far, axis=0))
    sums = [own, *sums]

    divisor = degree[:, None].astype(f32)
    self_part = dot(features, w_self) + bias_term
    layer_out, grad_pre, *packets = middle(
        1.0 / math.sqrt(node_total),
        jnp.reshape(c, (1,)),
        divisor,
        sums,
        self_part,
        features,
        w_neigh,
        grad_out,
    )
    packets = [packets[0]] + [swap_col(packets[k], k) for k in range(1, NC)]
    row_grads = jnp.concatenate([p[:nodes] for p in packets], axis=0)
    rider = add_up([p[nodes:] for p in packets])
    rider = (rider + swap_x(rider)).astype(bf16)

    def message(*blocks):
        return jnp.concatenate([block.astype(bf16) for block in blocks], axis=0)

    far = dot_t(dense_y[3], row_grads)
    down, up = message(far[:half]), message(far[half:])
    down, up, row_grads = lax.optimization_barrier((down, up, row_grads))
    down, up = shift_y(down, 1).astype(f32), shift_y(up, -1).astype(f32)
    terms_y = [dot_t(a, row_grads) for a in dense_y[:3]]
    late, down = lax.optimization_barrier((row_grads, down))
    terms_z = [dot_t(a, late if i == 5 else row_grads) for i, a in enumerate(dense_z)]
    wide = line_z.shape[0]
    down = shift_y(message(terms_y[2][:half] + down, terms_y[2][half:], rider), 1)
    up = shift_y(message(terms_y[1][:half], terms_y[1][half:] + up, rider), -1)
    rider = add_up([rider, up[wide:], shift_y(rider, 2), down[wide:]]).astype(bf16)
    down, up = down[:wide], up[:wide]
    back_z = terms_y[0] + down.astype(f32) + up.astype(f32)
    back_z = [back_z[i * nodes : (i + 1) * nodes] for i in range(NZ)]

    ring1 = shift_z(message(terms_z[7]), 1).astype(f32)
    down2 = shift_z(message(terms_z[6] + ring1), 1).astype(f32)
    up2 = shift_z(message(terms_z[5]), -1).astype(f32)
    down3 = shift_z(message(terms_z[4] + down2, back_z[6], rider), 1)
    up3 = shift_z(message(terms_z[3] + up2, back_z[5], rider), -1)
    far = shift_z(message(back_z[7]), 2).astype(f32)

    down3, up3 = lax.optimization_barrier((down3, up3))

    def split(got):
        return got[:size].astype(f32), got[size : size + nodes].astype(f32), got[size + nodes :]

    ring_d, block_d, rider_d1 = split(down3)
    ring_u, block_u, rider_u1 = split(up3)
    down4 = shift_z(message(terms_z[2] + ring_d, back_z[4] + block_d + far, rider_d1), 1)
    up4 = shift_z(message(terms_z[1] + ring_u, back_z[3] + block_u, rider_u1), -1)
    down4, up4 = lax.optimization_barrier((down4, up4))
    ring_d, block_d, rider_d2 = split(down4)
    ring_u, block_u, rider_u2 = split(up4)
    rider4 = shift_z(rider_d2, 2)
    back_y = terms_z[0] + ring_d + ring_u
    down5 = shift_z(message(back_z[2] + block_d, rider_d2), 1)
    up5 = shift_z(message(back_z[1] + block_u, rider_u2), -1)
    sum0 = back_z[0] + down5[:nodes].astype(f32) + up5[:nodes].astype(f32)
    rider_d3, rider_u3 = down5[nodes:], up5[nodes:]
    sum1 = back_y[:nodes]
    for i, d in enumerate(OFFSETS_Y[1:], 1):
        sum1 = sum1 + shift_y(message(back_y[i * nodes : (i + 1) * nodes]), d).astype(f32)

    total = add_up(
        [rider, rider_u1, rider_u2, rider_u3, rider4, rider_d3, rider_d2, rider_d1]
    )
    quarter = total[:nodes].astype(bf16)
    quarters = jnp.stack([quarter] + [swap_col(quarter, k) for k in range(1, NC)])
    grads = quarters[c ^ jnp.arange(NC, dtype=jnp.int32)].reshape(NC * nodes, width).astype(f32)

    kept = jnp.where(x == 0, sum0, sum1)
    sent = jnp.where(x == 0, sum1, sum0)
    neighbor_back = kept + swap_x(sent)
    grad_input = (dot(grad_pre, w_self.T) + neighbor_back).astype(bf16)
    return (layer_out, grad_input, grads[:width], grads[width:], total[nodes])


def solution(mesh):
    return jax.shard_map(
        shards,
        mesh=mesh,
        in_specs=(
            P(("row", "col"), None),
            P(("row", "col")),
            P("col", "row"),
            P("col", "row", None),
            P("col", "row", None),
            P("col", "row", None, None, None),
            P(),
            P(),
            P(),
            P(("row", "col"), None),
        ),
        out_specs=(P(("row", "col"), None), P(("row", "col"), None), P(), P(), P()),
        check_vma=False,
    )
```

```python
import functools
import math

import jax
import jax.numpy as jnp
from jax import lax
from jax.experimental import pallas as pl
from jax.experimental.pallas import tpu as pltpu
from jax.sharding import PartitionSpec as P

NY, NX, NZ, NC = 4, 2, 8, 4
TILE = 128
bf16, f32 = jnp.bfloat16, jnp.float32


def row_id(y, x, z):
    return (y % NY * NX + x % NX) * NZ + z % NZ


def row_perm(move):
    return [
        (row_id(y, x, z), row_id(*move(y, x, z)))
        for y in range(NY)
        for x in range(NX)
        for z in range(NZ)
    ]


def shift_z(a, d):
    return lax.ppermute(a, "row", row_perm(lambda y, x, z: (y, x, z + d)))


def shift_y(a, d):
    return lax.ppermute(a, "row", row_perm(lambda y, x, z: (y + d, x, z)))


def swap_x(a):
    return lax.ppermute(a, "row", row_perm(lambda y, x, z: (y, 1 - x, z)))


def swap_bits(a, name, size, bit):
    return lax.ppermute(a, name, [(i, i ^ bit) for i in range(size)])


def swap_col(a, bit):
    return swap_bits(a, "col", NC, bit)


OFFSETS_Y = (0, -1, 1, 2)


def ring_place(step, n):
    return jnp.where(step < n // 2, 2 * step, jnp.where(step == n // 2, n - 1, 2 * (n - step) - 1))


PIECES = NY + NZ
REPEATS = 16 * 32


def plan_tiles(tile_count, tile_rows, tile_cols):
    r, c = lax.axis_index("row"), lax.axis_index("col")
    z, x, y = r % NZ, r // NZ % NX, r // (NZ * NX)
    count, rows, cols = tile_count[0, 0], tile_rows[0, 0], tile_cols[0, 0]
    zi = ring_place((cols % NZ - z) % NZ, NZ)
    yi = ring_place((cols // (NZ * NX) - y) % NY, NY)
    u = rows ^ c
    slots = jnp.arange(rows.shape[0], dtype=jnp.int32)
    key = jnp.where(
        cols // NZ % NX == 0, yi * 32 + u * NZ + zi, (NY + zi) * 32 + u * NY + yi
    )
    live = slots < count
    same = (key[None, :] == key[:, None]) & (slots[None, :] < slots[:, None]) & live[None, :]
    repeat = jnp.any(same, axis=1)
    key = jnp.where(live, jnp.where(repeat, key + REPEATS, key), 2 * REPEATS)
    order = key * rows.shape[0] + slots
    rank = jnp.sum((order[None, :] < order[:, None]).astype(jnp.int32), axis=1)
    listed = jnp.sum(jnp.where(rank[:, None] == slots[None, :], order[:, None], 0), axis=0)
    edges = jnp.arange(32, dtype=jnp.int32) * 32
    starts = jnp.sum((key[None, :] < edges[:, None]).astype(jnp.int32), axis=1)
    return starts, listed


def dense_kernel(pieces, starts, listed, values, after, *rest):
    outs, total = rest[:-1], rest[-1]
    slot_count = listed.shape[0]

    def window(out, entry):
        wide = out.shape[1] // TILE
        place = (entry // slot_count) & 31
        u, v = place // wide, place & (wide - 1)
        return out.at[pl.ds(pl.multiple_of(u * TILE, TILE), TILE), pl.ds(pl.multiple_of(v * TILE, TILE), TILE)]

    for piece, out in zip(pieces, outs):

        def clear(i, carry):
            out[pl.ds(pl.multiple_of(i * 64, 64), 64), :] = jnp.zeros((64, out.shape[1]), bf16)
            return carry

        def place_first(j, carry):
            entry = listed[j]
            window(out, entry)[...] = values[entry & (slot_count - 1)]
            return carry

        def add(j, carry):
            entry = listed[j]
            cell = entry // slot_count
            spot = window(out, entry)
            base = jnp.where(cell == carry, total[...], spot[...].astype(f32))
            value = base + values[entry & (slot_count - 1)].astype(f32)
            total[...] = value
            spot[...] = value.astype(bf16)
            return cell

        lax.fori_loop(0, out.shape[0] // 64, clear, 0)
        lax.fori_loop(starts[piece], starts[piece + 1], place_first, 0)
        again = REPEATS // 32 + piece
        lax.fori_loop(starts[again], starts[again + 1], add, -1)


VMEM = pl.BlockSpec(memory_space=pltpu.VMEM)
SMEM = pl.BlockSpec(memory_space=pltpu.SMEM)


def dense_pieces(pieces, starts, listed, values, after):
    shapes = [
        jax.ShapeDtypeStruct((NC * TILE, (NZ if p < NY else NY) * TILE), bf16)
        for p in pieces
    ]
    return pl.pallas_call(
        functools.partial(dense_kernel, pieces),
        out_shape=shapes,
        in_specs=[SMEM, SMEM, VMEM, pl.BlockSpec(memory_space=pl.ANY)],
        out_specs=[VMEM] * len(pieces),
        scratch_shapes=[pltpu.VMEM((TILE, TILE), f32)],
        compiler_params=pltpu.CompilerParams(vmem_limit_bytes=4 * 2**20),
        cost_estimate=pl.CostEstimate(flops=4 * 10**6, bytes_accessed=10 * 2**20, transcendentals=0),
        name=f"dense{pieces[0]}",
    )(starts, listed, values, after)


def last_dot_kernel(so_far, weights, near, far, *outs):
    half = near.shape[0]
    for k, out in enumerate(outs, 1):
        rows = slice(k * TILE, (k + 1) * TILE)
        out[...] = (
            so_far[rows, :] + dot(weights[rows, :half], near[...]) + dot(weights[rows, half:], far[...])
        ).astype(out.dtype)


def last_dot(so_far, weights, near, far, types):
    shape = (TILE, so_far.shape[1])
    return pl.pallas_call(
        last_dot_kernel,
        out_shape=[jax.ShapeDtypeStruct(shape, t) for t in types],
        in_specs=[VMEM] * 4,
        out_specs=[VMEM] * len(types),
        compiler_params=pltpu.CompilerParams(vmem_limit_bytes=8 * 2**20),
        cost_estimate=pl.CostEstimate(flops=3 * 10**8, bytes_accessed=2 * 2**20, transcendentals=0),
        name="last_dot",
    )(so_far, weights, near, far)


def middle_kernel(scale, place, divisor, *rest):
    inputs, (layer_out, grad_pre), rest = rest[:8], rest[8:10], rest[10:]
    packets, held, (local, layer_held, sems) = rest[:NC], rest[NC : NC + 8], rest[NC + 8 :]
    copies = [
        pltpu.make_async_copy(source, target, sems.at[i])
        for i, (source, target) in enumerate(zip(inputs, held))
    ]
    for copy in copies:
        copy.start()
    for copy in copies:
        copy.wait()
    own, got1, got2, got3, self_part, features, w_neigh, grad_out = held
    nodes, width = features.shape
    agg_sum = own[...] + got1[...] + got2[...].astype(f32) + got3[...].astype(f32)
    aggregate = (agg_sum / divisor[...]).astype(bf16)
    pre_act = self_part[...] + dot(aggregate, w_neigh[...])
    sigmoid_pre = jax.nn.sigmoid(pre_act)
    layer_held[...] = (pre_act * sigmoid_pre).astype(bf16)
    leave = pltpu.make_async_copy(layer_held, layer_out, sems.at[8])
    leave.start()
    grad = (
        grad_out[...].astype(f32) * (sigmoid_pre * (1.0 + pre_act * (1.0 - sigmoid_pre)))
    ).astype(bf16)
    grad_pre[...] = grad
    back = lax.dot_general(
        grad, w_neigh[...], (((1,), (1,)), ((), ())), preferred_element_type=f32
    )
    scaled = (back / divisor[...]).astype(bf16)
    local[:width, :] = (dot_t(features[...], grad) * scale).astype(bf16)
    local[width:, :] = (dot_t(aggregate, grad) * scale).astype(bf16)
    bias = jnp.sum(grad.astype(f32), axis=0, keepdims=True) * scale
    bias = jnp.where(lax.broadcasted_iota(jnp.int32, (16, width), 0) == 0, bias, 0.0).astype(bf16)
    for k, packet in enumerate(packets):
        packet[:nodes, :] = scaled
        start = pl.multiple_of((place[0] ^ k) * nodes, nodes)
        packet[nodes : 2 * nodes, :] = local[pl.ds(start, nodes), :]
        packet[2 * nodes :, :] = bias
    leave.wait()


def middle(scale, place, divisor, sums, self_part, features, w_neigh, grad_out):
    nodes, width = features.shape
    inputs = [*sums, self_part, features, w_neigh, grad_out]
    node_shape = jax.ShapeDtypeStruct((nodes, width), bf16)
    packet_shape = jax.ShapeDtypeStruct((2 * nodes + 16, width), bf16)
    anywhere = pl.BlockSpec(memory_space=pl.ANY)
    return pl.pallas_call(
        functools.partial(middle_kernel, scale),
        out_shape=[node_shape] * 2 + [packet_shape] * NC,
        in_specs=[SMEM, VMEM] + [anywhere] * 8,
        out_specs=[anywhere, VMEM] + [VMEM] * NC,
        scratch_shapes=[pltpu.VMEM(a.shape, a.dtype) for a in inputs]
        + [
            pltpu.VMEM((2 * width, width), bf16),
            pltpu.VMEM((nodes, width), bf16),
            pltpu.SemaphoreType.DMA((9,)),
        ],
        compiler_params=pltpu.CompilerParams(vmem_limit_bytes=8 * 2**20),
        cost_estimate=pl.CostEstimate(flops=10**8, bytes_accessed=2 * 2**20, transcendentals=nodes * width),
        name="middle",
    )(place, divisor, *inputs)


def dot(a, b):
    return jnp.dot(a, b, preferred_element_type=f32)


def dot_t(a, b):
    return lax.dot_general(a, b, (((0,), (0,)), ((), ())), preferred_element_type=f32)


def add_up(parts):
    parts = [p.astype(f32) for p in parts]
    while len(parts) > 1:
        half = len(parts) // 2
        parts = [a + b for a, b in zip(parts[:half], parts[half:])]
    return parts[0]


def shards(
    features,
    degree,
    tile_count,
    tile_rows,
    tile_cols,
    tile_values,
    w_self,
    w_neigh,
    bias_term,
    grad_out,
):
    r, c = lax.axis_index("row"), lax.axis_index("col")
    x = r // NZ % NX
    nodes, width = features.shape
    node_total = nodes * NY * NX * NZ * NC

    starts, listed = plan_tiles(tile_count, tile_rows, tile_cols)
    values = tile_values[0, 0]

    other = swap_x(features)
    block0 = jnp.where(x == 0, features, other)
    block1 = jnp.where(x == 0, other, features)
    down1, up1 = shift_z(block0, 1), shift_z(block0, -1)
    line_y = jnp.concatenate(
        [block1, shift_y(block1, 1), shift_y(block1, -1), shift_y(block1, 2)], axis=0
    )
    size = line_y.shape[0]
    down2 = shift_z(jnp.concatenate([line_y, down1], axis=0), 1)
    up2 = shift_z(jnp.concatenate([line_y, up1], axis=0), -1)
    down3, up3 = shift_z(down2, 1), shift_z(up2, -1)
    far = shift_z(down2[size:], 2)
    line_a = jnp.concatenate([block0, down1, up1], axis=0)
    line_b = jnp.concatenate(
        [down2[size:], up2[size:], down3[size:], up3[size:], far], axis=0
    )
    cut, half = line_a.shape[0], NZ // 2 * nodes
    down_a, up_a = shift_y(line_a, 1), shift_y(line_a, -1)
    down_b, up_b = shift_y(line_b, 1), shift_y(line_b, -1)
    far = (
        shift_y(jnp.concatenate([down_a, down_b[: half - cut]], axis=0), 1),
        shift_y(up_b[half - cut :], -1),
    )
    down4, up4 = shift_z(down3[:size], 1), shift_z(up3[:size], -1)
    down5 = shift_z(down4, 1)
    plane_z = [line_y, down2[:size], up2[:size], down3[:size], up3[:size], down4, up4, down5]
    dense_z = dense_pieces(range(NY, PIECES), starts, listed, values, up2)
    dense_y = dense_pieces(range(NY), starts, listed, values, up_a)

    so_far = None
    pairs = [(dense_y[i][:, :cut], block) for i, block in enumerate((line_a, down_a, up_a))]
    pairs += [(dense_y[i][:, cut:], block) for i, block in enumerate((line_b, down_b, up_b))]
    for a, b in pairs + list(zip(dense_z, plane_z)):
        so_far = dot(a, b) if so_far is None else so_far + dot(a, b)
    sent = last_dot(so_far, dense_y[3], *far, [f32, bf16, bf16])
    sums = [swap_col(block, k) for k, block in enumerate(sent, 1)]
    own = so_far[:nodes] + dot(dense_y[3][:nodes], jnp.concatenate(far, axis=0))
    sums = [own, *sums]

    divisor = degree[:, None].astype(f32)
    self_part = dot(features, w_self) + bias_term
    layer_out, grad_pre, *packets = middle(
        1.0 / math.sqrt(node_total),
        jnp.reshape(c, (1,)),
        divisor,
        sums,
        self_part,
        features,
        w_neigh,
        grad_out,
    )
    packets = [packets[0]] + [swap_col(packets[k], k) for k in range(1, NC)]
    row_grads = jnp.concatenate([p[:nodes] for p in packets], axis=0)
    rider = add_up([p[nodes:] for p in packets])
    rider = (rider + swap_x(rider)).astype(bf16)

    def message(*blocks):
        return jnp.concatenate([block.astype(bf16) for block in blocks], axis=0)

    far = dot_t(dense_y[3], row_grads)
    down, up = message(far[:half]), message(far[half:])
    down, up, row_grads = lax.optimization_barrier((down, up, row_grads))
    down, up = shift_y(down, 1).astype(f32), shift_y(up, -1).astype(f32)
    terms_y = [dot_t(a, row_grads) for a in dense_y[:3]]
    late, late_rider, down = lax.optimization_barrier((row_grads, rider, down))
    terms_z = [dot_t(a, late if i == 5 else row_grads) for i, a in enumerate(dense_z)]
    top, down = down[:cut], down[cut:]
    before, after = terms_y[1], terms_y[2]
    down_b = shift_y(message(after[cut:half] + down, after[half:], rider), 1)
    up_b = shift_y(message(before[cut:half], before[half:] + up, rider), -1)
    down_b, up_b, top, rest = lax.optimization_barrier(
        (down_b, up_b, message(after[:cut] + top), message(before[:cut]))
    )
    down_a, up_a = shift_y(top, 1), shift_y(rest, -1)
    wide = NZ * nodes - cut
    rider = add_up([rider, up_b[wide:], shift_y(late_rider, 2), down_b[wide:]]).astype(bf16)
    back_z = [
        terms_y[0][:cut] + down_a.astype(f32) + up_a.astype(f32),
        terms_y[0][cut:] + down_b[:wide].astype(f32) + up_b[:wide].astype(f32),
    ]
    back_z = [part[i : i + nodes] for part in back_z for i in range(0, part.shape[0], nodes)]

    ring1 = shift_z(message(terms_z[7]), 1).astype(f32)
    down2 = shift_z(message(terms_z[6] + ring1), 1).astype(f32)
    up2 = shift_z(message(terms_z[5]), -1).astype(f32)
    down3 = shift_z(message(terms_z[4] + down2, back_z[6], rider), 1)
    up3 = shift_z(message(terms_z[3] + up2, back_z[5], rider), -1)
    far = shift_z(message(back_z[7]), 2).astype(f32)

    down3, up3 = lax.optimization_barrier((down3, up3))

    def split(got):
        return got[:size].astype(f32), got[size : size + nodes].astype(f32), got[size + nodes :]

    ring_d, block_d, rider_d1 = split(down3)
    ring_u, block_u, rider_u1 = split(up3)
    down4 = shift_z(message(terms_z[2] + ring_d, back_z[4] + block_d + far, rider_d1), 1)
    up4 = shift_z(message(terms_z[1] + ring_u, back_z[3] + block_u, rider_u1), -1)
    down4, up4 = lax.optimization_barrier((down4, up4))
    ring_d, block_d, rider_d2 = split(down4)
    ring_u, block_u, rider_u2 = split(up4)
    rider4 = shift_z(rider_d2, 2)
    back_y = terms_z[0] + ring_d + ring_u
    down5 = shift_z(message(back_z[2] + block_d, rider_d2), 1)
    up5 = shift_z(message(back_z[1] + block_u, rider_u2), -1)
    sum0 = back_z[0] + down5[:nodes].astype(f32) + up5[:nodes].astype(f32)
    rider_d3, rider_u3 = down5[nodes:], up5[nodes:]
    sum1 = back_y[:nodes]
    for i, d in enumerate(OFFSETS_Y[1:], 1):
        sum1 = sum1 + shift_y(message(back_y[i * nodes : (i + 1) * nodes]), d).astype(f32)

    total = add_up(
        [rider, rider_u1, rider_u2, rider_u3, rider4, rider_d3, rider_d2, rider_d1]
    )
    quarter = total[:nodes].astype(bf16)
    quarters = jnp.stack([quarter] + [swap_col(quarter, k) for k in range(1, NC)])
    grads = quarters[c ^ jnp.arange(NC, dtype=jnp.int32)].reshape(NC * nodes, width).astype(f32)

    kept = jnp.where(x == 0, sum0, sum1)
    sent = jnp.where(x == 0, sum1, sum0)
    neighbor_back = kept + swap_x(sent)
    grad_input = (dot(grad_pre, w_self.T) + neighbor_back).astype(bf16)
    return (layer_out, grad_input, grads[:width], grads[width:], total[nodes])


def solution(mesh):
    return jax.shard_map(
        shards,
        mesh=mesh,
        in_specs=(
            P(("row", "col"), None),
            P(("row", "col")),
            P("col", "row"),
            P("col", "row", None),
            P("col", "row", None),
            P("col", "row", None, None, None),
            P(),
            P(),
            P(),
            P(("row", "col"), None),
        ),
        out_specs=(P(("row", "col"), None), P(("row", "col"), None), P(), P(), P()),
        check_vma=False,
    )
```

```python
import functools
import math

import jax
import jax.numpy as jnp
from jax import lax
from jax.experimental import pallas as pl
from jax.experimental.pallas import tpu as pltpu
from jax.sharding import PartitionSpec as P

NY, NX, NZ, NC = 4, 2, 8, 4
TILE = 128
bf16, f32 = jnp.bfloat16, jnp.float32


def row_id(y, x, z):
    return (y % NY * NX + x % NX) * NZ + z % NZ


def row_perm(move):
    return [
        (row_id(y, x, z), row_id(*move(y, x, z)))
        for y in range(NY)
        for x in range(NX)
        for z in range(NZ)
    ]


def shift_z(a, d):
    return lax.ppermute(a, "row", row_perm(lambda y, x, z: (y, x, z + d)))


def shift_y(a, d):
    return lax.ppermute(a, "row", row_perm(lambda y, x, z: (y + d, x, z)))


def swap_x(a):
    return lax.ppermute(a, "row", row_perm(lambda y, x, z: (y, 1 - x, z)))


def swap_bits(a, name, size, bit):
    return lax.ppermute(a, name, [(i, i ^ bit) for i in range(size)])


def swap_col(a, bit):
    return swap_bits(a, "col", NC, bit)


OFFSETS_Y = (0, -1, 1, 2)


def ring_place(step, n):
    return jnp.where(step < n // 2, 2 * step, jnp.where(step == n // 2, n - 1, 2 * (n - step) - 1))


PIECES = NY + NZ
REPEATS = 16 * 32


def plan_tiles(tile_count, tile_rows, tile_cols):
    r, c = lax.axis_index("row"), lax.axis_index("col")
    z, x, y = r % NZ, r // NZ % NX, r // (NZ * NX)
    count, rows, cols = tile_count[0, 0], tile_rows[0, 0], tile_cols[0, 0]
    zi = ring_place((cols % NZ - z) % NZ, NZ)
    yi = ring_place((cols // (NZ * NX) - y) % NY, NY)
    u = rows ^ c
    slots = jnp.arange(rows.shape[0], dtype=jnp.int32)
    key = jnp.where(
        cols // NZ % NX == 0, yi * 32 + u * NZ + zi, (NY + zi) * 32 + u * NY + yi
    )
    live = slots < count
    same = (key[None, :] == key[:, None]) & (slots[None, :] < slots[:, None]) & live[None, :]
    repeat = jnp.any(same, axis=1)
    key = jnp.where(live, jnp.where(repeat, key + REPEATS, key), 2 * REPEATS)
    order = key * rows.shape[0] + slots
    rank = jnp.sum((order[None, :] < order[:, None]).astype(jnp.int32), axis=1)
    listed = jnp.sum(jnp.where(rank[:, None] == slots[None, :], order[:, None], 0), axis=0)
    edges = jnp.arange(32, dtype=jnp.int32) * 32
    starts = jnp.sum((key[None, :] < edges[:, None]).astype(jnp.int32), axis=1)
    return starts, listed


def dense_kernel(pieces, starts, listed, values, after, *rest):
    outs, total = rest[:-1], rest[-1]
    slot_count = listed.shape[0]

    def window(out, entry):
        wide = out.shape[1] // TILE
        place = (entry // slot_count) & 31
        u, v = place // wide, place & (wide - 1)
        return out.at[pl.ds(pl.multiple_of(u * TILE, TILE), TILE), pl.ds(pl.multiple_of(v * TILE, TILE), TILE)]

    for piece, out in zip(pieces, outs):

        def clear(i, carry):
            out[pl.ds(pl.multiple_of(i * 64, 64), 64), :] = jnp.zeros((64, out.shape[1]), bf16)
            return carry

        def place_first(j, carry):
            entry = listed[j]
            window(out, entry)[...] = values[entry & (slot_count - 1)]
            return carry

        def add(j, carry):
            entry = listed[j]
            cell = entry // slot_count
            spot = window(out, entry)
            base = jnp.where(cell == carry, total[...], spot[...].astype(f32))
            value = base + values[entry & (slot_count - 1)].astype(f32)
            total[...] = value
            spot[...] = value.astype(bf16)
            return cell

        lax.fori_loop(0, out.shape[0] // 64, clear, 0)
        lax.fori_loop(starts[piece], starts[piece + 1], place_first, 0)
        again = REPEATS // 32 + piece
        lax.fori_loop(starts[again], starts[again + 1], add, -1)


VMEM = pl.BlockSpec(memory_space=pltpu.VMEM)
SMEM = pl.BlockSpec(memory_space=pltpu.SMEM)


def dense_pieces(pieces, starts, listed, values, after):
    shapes = [
        jax.ShapeDtypeStruct((NC * TILE, (NZ if p < NY else NY) * TILE), bf16)
        for p in pieces
    ]
    return pl.pallas_call(
        functools.partial(dense_kernel, pieces),
        out_shape=shapes,
        in_specs=[SMEM, SMEM, VMEM, pl.BlockSpec(memory_space=pl.ANY)],
        out_specs=[VMEM] * len(pieces),
        scratch_shapes=[pltpu.VMEM((TILE, TILE), f32)],
        compiler_params=pltpu.CompilerParams(vmem_limit_bytes=4 * 2**20),
        cost_estimate=pl.CostEstimate(flops=4 * 10**6, bytes_accessed=10 * 2**20, transcendentals=0),
        name=f"dense{pieces[0]}",
    )(starts, listed, values, after)


def last_dot_kernel(so_far, weights, near, far, *outs):
    half = near.shape[0]
    for k, out in enumerate(outs, 1):
        rows = slice(k * TILE, (k + 1) * TILE)
        out[...] = (
            so_far[rows, :] + dot(weights[rows, :half], near[...]) + dot(weights[rows, half:], far[...])
        ).astype(out.dtype)


def last_dot(so_far, weights, near, far, types):
    shape = (TILE, so_far.shape[1])
    return pl.pallas_call(
        last_dot_kernel,
        out_shape=[jax.ShapeDtypeStruct(shape, t) for t in types],
        in_specs=[VMEM] * 4,
        out_specs=[VMEM] * len(types),
        compiler_params=pltpu.CompilerParams(vmem_limit_bytes=8 * 2**20),
        cost_estimate=pl.CostEstimate(flops=3 * 10**8, bytes_accessed=2 * 2**20, transcendentals=0),
        name="last_dot",
    )(so_far, weights, near, far)


def middle_kernel(scale, place, divisor, *rest):
    inputs, (layer_out, grad_pre), rest = rest[:8], rest[8:10], rest[10:]
    packets, held, (local, layer_held, sems) = rest[:NC], rest[NC : NC + 8], rest[NC + 8 :]
    copies = [
        pltpu.make_async_copy(source, target, sems.at[i])
        for i, (source, target) in enumerate(zip(inputs, held))
    ]
    for copy in copies:
        copy.start()
    for copy in copies:
        copy.wait()
    own, got1, got2, got3, self_part, features, w_neigh, grad_out = held
    nodes, width = features.shape
    agg_sum = own[...] + got1[...] + got2[...].astype(f32) + got3[...].astype(f32)
    aggregate = (agg_sum / divisor[...]).astype(bf16)
    pre_act = self_part[...] + dot(aggregate, w_neigh[...])
    sigmoid_pre = jax.nn.sigmoid(pre_act)
    layer_held[...] = (pre_act * sigmoid_pre).astype(bf16)
    leave = pltpu.make_async_copy(layer_held, layer_out, sems.at[8])
    leave.start()
    grad = (
        grad_out[...].astype(f32) * (sigmoid_pre * (1.0 + pre_act * (1.0 - sigmoid_pre)))
    ).astype(bf16)
    grad_pre[...] = grad
    back = lax.dot_general(
        grad, w_neigh[...], (((1,), (1,)), ((), ())), preferred_element_type=f32
    )
    scaled = (back / divisor[...]).astype(bf16)
    local[:width, :] = (dot_t(features[...], grad) * scale).astype(bf16)
    local[width:, :] = (dot_t(aggregate, grad) * scale).astype(bf16)
    bias = jnp.sum(grad.astype(f32), axis=0, keepdims=True) * scale
    bias = jnp.where(lax.broadcasted_iota(jnp.int32, (16, width), 0) == 0, bias, 0.0).astype(bf16)
    for k, packet in enumerate(packets):
        packet[:nodes, :] = scaled
        start = pl.multiple_of((place[0] ^ k) * nodes, nodes)
        packet[nodes : 2 * nodes, :] = local[pl.ds(start, nodes), :]
        packet[2 * nodes :, :] = bias
    leave.wait()


def middle(scale, place, divisor, sums, self_part, features, w_neigh, grad_out):
    nodes, width = features.shape
    inputs = [*sums, self_part, features, w_neigh, grad_out]
    node_shape = jax.ShapeDtypeStruct((nodes, width), bf16)
    packet_shape = jax.ShapeDtypeStruct((2 * nodes + 16, width), bf16)
    anywhere = pl.BlockSpec(memory_space=pl.ANY)
    return pl.pallas_call(
        functools.partial(middle_kernel, scale),
        out_shape=[node_shape] * 2 + [packet_shape] * NC,
        in_specs=[SMEM, VMEM] + [anywhere] * 8,
        out_specs=[anywhere, VMEM] + [VMEM] * NC,
        scratch_shapes=[pltpu.VMEM(a.shape, a.dtype) for a in inputs]
        + [
            pltpu.VMEM((2 * width, width), bf16),
            pltpu.VMEM((nodes, width), bf16),
            pltpu.SemaphoreType.DMA((9,)),
        ],
        compiler_params=pltpu.CompilerParams(vmem_limit_bytes=8 * 2**20),
        cost_estimate=pl.CostEstimate(flops=10**8, bytes_accessed=2 * 2**20, transcendentals=nodes * width),
        name="middle",
    )(place, divisor, *inputs)


def dot(a, b):
    return jnp.dot(a, b, preferred_element_type=f32)


def dot_t(a, b):
    return lax.dot_general(a, b, (((0,), (0,)), ((), ())), preferred_element_type=f32)


def add_up(parts):
    parts = [p.astype(f32) for p in parts]
    while len(parts) > 1:
        half = len(parts) // 2
        parts = [a + b for a, b in zip(parts[:half], parts[half:])]
    return parts[0]


def shards(
    features,
    degree,
    tile_count,
    tile_rows,
    tile_cols,
    tile_values,
    w_self,
    w_neigh,
    bias_term,
    grad_out,
):
    r, c = lax.axis_index("row"), lax.axis_index("col")
    x = r // NZ % NX
    nodes, width = features.shape
    node_total = nodes * NY * NX * NZ * NC

    starts, listed = plan_tiles(tile_count, tile_rows, tile_cols)
    values = tile_values[0, 0]

    other = swap_x(features)
    block0 = jnp.where(x == 0, features, other)
    block1 = jnp.where(x == 0, other, features)
    down1, up1 = shift_z(block0, 1), shift_z(block0, -1)
    line_y = jnp.concatenate(
        [block1, shift_y(block1, 1), shift_y(block1, -1), shift_y(block1, 2)], axis=0
    )
    size = line_y.shape[0]
    line_a = jnp.concatenate([block0, down1, up1], axis=0)
    down2 = shift_z(jnp.concatenate([line_y, down1], axis=0), 1)
    up2 = shift_z(jnp.concatenate([line_y, up1], axis=0), -1)
    down3, up3 = shift_z(down2, 1), shift_z(up2, -1)
    far = shift_z(down2[size:], 2)
    line_b = jnp.concatenate(
        [down2[size:], up2[size:], down3[size:], up3[size:], far], axis=0
    )
    cut, half = line_a.shape[0], NZ // 2 * nodes
    down_a, up_a = shift_y(line_a, 1), shift_y(line_a, -1)
    down_b, up_b = shift_y(line_b, 1), shift_y(line_b, -1)
    far = (
        shift_y(jnp.concatenate([down_a, down_b[: half - cut]], axis=0), 1),
        shift_y(up_b[half - cut :], -1),
    )
    down4, up4 = shift_z(down3[:size], 1), shift_z(up3[:size], -1)
    down5 = shift_z(down4, 1)
    plane_z = [line_y, down2[:size], up2[:size], down3[:size], up3[:size], down4, up4, down5]
    dense_z = dense_pieces(range(NY, PIECES), starts, listed, values, up2)
    dense_y = dense_pieces(range(NY), starts, listed, values, up_a)

    so_far = None
    pairs = [(dense_y[i][:, :cut], block) for i, block in enumerate((line_a, down_a, up_a))]
    pairs += [(dense_y[i][:, cut:], block) for i, block in enumerate((line_b, down_b, up_b))]
    for a, b in pairs + list(zip(dense_z, plane_z)):
        so_far = dot(a, b) if so_far is None else so_far + dot(a, b)
    sent = last_dot(so_far, dense_y[3], *far, [f32, bf16, bf16])
    sums = [swap_col(block, k) for k, block in enumerate(sent, 1)]
    own = so_far[:nodes] + dot(dense_y[3][:nodes], jnp.concatenate(far, axis=0))
    sums = [own, *sums]

    divisor = degree[:, None].astype(f32)
    self_part = dot(features, w_self) + bias_term
    layer_out, grad_pre, *packets = middle(
        1.0 / math.sqrt(node_total),
        jnp.reshape(c, (1,)),
        divisor,
        sums,
        self_part,
        features,
        w_neigh,
        grad_out,
    )
    packets = [packets[0]] + [swap_col(packets[k], k) for k in range(1, NC)]
    row_grads = jnp.concatenate([p[:nodes] for p in packets], axis=0)
    rider = add_up([p[nodes:] for p in packets])
    rider = (rider + swap_x(rider)).astype(bf16)

    def message(*blocks):
        return jnp.concatenate([block.astype(bf16) for block in blocks], axis=0)

    far = dot_t(dense_y[3], row_grads)
    down, up = message(far[:half]), message(far[half:])
    down, up, row_grads = lax.optimization_barrier((down, up, row_grads))
    down, up = shift_y(down, 1).astype(f32), shift_y(up, -1).astype(f32)
    terms_y = [dot_t(a, row_grads) for a in dense_y[:3]]
    top, down = down[:cut], down[cut:]
    before, after = terms_y[1], terms_y[2]
    down_b = message(after[cut:half] + down, after[half:], rider)
    up_b = message(before[cut:half], before[half:] + up, rider)
    down_b, up_b, late, late_rider = lax.optimization_barrier((down_b, up_b, row_grads, rider))
    terms_z = [dot_t(a, late if i in (5, 6) else row_grads) for i, a in enumerate(dense_z)]
    down_b, up_b = shift_y(down_b, 1), shift_y(up_b, -1)
    down_b, up_b, top, rest = lax.optimization_barrier(
        (down_b, up_b, message(after[:cut] + top), message(before[:cut]))
    )
    down_a, up_a = shift_y(top, 1), shift_y(rest, -1)
    wide = NZ * nodes - cut
    rider = add_up([rider, up_b[wide:], shift_y(late_rider, 2), down_b[wide:]]).astype(bf16)
    back_z = [
        terms_y[0][:cut] + down_a.astype(f32) + up_a.astype(f32),
        terms_y[0][cut:] + down_b[:wide].astype(f32) + up_b[:wide].astype(f32),
    ]
    back_z = [part[i : i + nodes] for part in back_z for i in range(0, part.shape[0], nodes)]

    ring1 = shift_z(message(terms_z[7]), 1).astype(f32)
    down2 = shift_z(message(terms_z[6] + ring1), 1).astype(f32)
    up2 = shift_z(message(terms_z[5]), -1).astype(f32)
    down3 = shift_z(message(terms_z[4] + down2, back_z[6], rider), 1)
    up3 = shift_z(message(terms_z[3] + up2, back_z[5], rider), -1)
    far = shift_z(message(back_z[7]), 2).astype(f32)

    down3, up3 = lax.optimization_barrier((down3, up3))

    def split(got):
        return got[:size].astype(f32), got[size : size + nodes].astype(f32), got[size + nodes :]

    ring_d, block_d, rider_d1 = split(down3)
    ring_u, block_u, rider_u1 = split(up3)
    down4 = shift_z(message(terms_z[2] + ring_d, back_z[4] + block_d + far, rider_d1), 1)
    up4 = shift_z(message(terms_z[1] + ring_u, back_z[3] + block_u, rider_u1), -1)
    down4, up4 = lax.optimization_barrier((down4, up4))
    ring_d, block_d, rider_d2 = split(down4)
    ring_u, block_u, rider_u2 = split(up4)
    rider4 = shift_z(rider_d2, 2)
    back_y = terms_z[0] + ring_d + ring_u
    down5 = shift_z(message(back_z[2] + block_d, rider_d2), 1)
    up5 = shift_z(message(back_z[1] + block_u, rider_u2), -1)
    sum0 = back_z[0] + down5[:nodes].astype(f32) + up5[:nodes].astype(f32)
    rider_d3, rider_u3 = down5[nodes:], up5[nodes:]
    sum1 = back_y[:nodes]
    for i, d in enumerate(OFFSETS_Y[1:], 1):
        sum1 = sum1 + shift_y(message(back_y[i * nodes : (i + 1) * nodes]), d).astype(f32)

    total = add_up(
        [rider, rider_u1, rider_u2, rider_u3, rider4, rider_d3, rider_d2, rider_d1]
    )
    quarter = total[:nodes].astype(bf16)
    quarters = [quarter] + [swap_col(quarter, k) for k in range(1, NC)]

    def rows_of(a):
        chosen = quarters[a]
        for k in range(1, NC):
            chosen = jnp.where(c == k, quarters[a ^ k], chosen)
        return chosen.astype(f32)

    grad_self = jnp.concatenate([rows_of(0), rows_of(1)], axis=0)
    grad_neigh = jnp.concatenate([rows_of(2), rows_of(3)], axis=0)

    kept = jnp.where(x == 0, sum0, sum1)
    sent = jnp.where(x == 0, sum1, sum0)
    neighbor_back = kept + swap_x(sent)
    grad_input = (dot(grad_pre, w_self.T) + neighbor_back).astype(bf16)
    return (layer_out, grad_input, grad_self, grad_neigh, total[nodes])


def solution(mesh):
    return jax.shard_map(
        shards,
        mesh=mesh,
        in_specs=(
            P(("row", "col"), None),
            P(("row", "col")),
            P("col", "row"),
            P("col", "row", None),
            P("col", "row", None),
            P("col", "row", None, None, None),
            P(),
            P(),
            P(),
            P(("row", "col"), None),
        ),
        out_specs=(P(("row", "col"), None), P(("row", "col"), None), P(), P(), P()),
        check_vma=False,
    )
```

```python
import functools
import math

import jax
import jax.numpy as jnp
from jax import lax
from jax.experimental import pallas as pl
from jax.experimental.pallas import tpu as pltpu
from jax.sharding import PartitionSpec as P

NY, NX, NZ, NC = 4, 2, 8, 4
TILE = 128
bf16, f32 = jnp.bfloat16, jnp.float32


def row_id(y, x, z):
    return (y % NY * NX + x % NX) * NZ + z % NZ


def row_perm(move):
    return [
        (row_id(y, x, z), row_id(*move(y, x, z)))
        for y in range(NY)
        for x in range(NX)
        for z in range(NZ)
    ]


def shift_z(a, d):
    return lax.ppermute(a, "row", row_perm(lambda y, x, z: (y, x, z + d)))


def shift_y(a, d):
    return lax.ppermute(a, "row", row_perm(lambda y, x, z: (y + d, x, z)))


def swap_x(a):
    return lax.ppermute(a, "row", row_perm(lambda y, x, z: (y, 1 - x, z)))


def swap_bits(a, name, size, bit):
    return lax.ppermute(a, name, [(i, i ^ bit) for i in range(size)])


def swap_col(a, bit):
    return swap_bits(a, "col", NC, bit)


OFFSETS_Y = (0, -1, 1, 2)


def ring_place(step, n):
    return jnp.where(step < n // 2, 2 * step, jnp.where(step == n // 2, n - 1, 2 * (n - step) - 1))


PIECES = NY + NZ
REPEATS = 16 * 32


def plan_tiles(tile_count, tile_rows, tile_cols):
    r, c = lax.axis_index("row"), lax.axis_index("col")
    z, x, y = r % NZ, r // NZ % NX, r // (NZ * NX)
    count, rows, cols = tile_count[0, 0], tile_rows[0, 0], tile_cols[0, 0]
    zi = ring_place((cols % NZ - z) % NZ, NZ)
    yi = ring_place((cols // (NZ * NX) - y) % NY, NY)
    u = rows ^ c
    slots = jnp.arange(rows.shape[0], dtype=jnp.int32)
    key = jnp.where(
        cols // NZ % NX == 0, yi * 32 + u * NZ + zi, (NY + zi) * 32 + u * NY + yi
    )
    live = slots < count
    same = (key[None, :] == key[:, None]) & (slots[None, :] < slots[:, None]) & live[None, :]
    repeat = jnp.any(same, axis=1)
    key = jnp.where(live, jnp.where(repeat, key + REPEATS, key), 2 * REPEATS)
    order = key * rows.shape[0] + slots
    rank = jnp.sum((order[None, :] < order[:, None]).astype(jnp.int32), axis=1)
    listed = jnp.sum(jnp.where(rank[:, None] == slots[None, :], order[:, None], 0), axis=0)
    edges = jnp.arange(32, dtype=jnp.int32) * 32
    starts = jnp.sum((key[None, :] < edges[:, None]).astype(jnp.int32), axis=1)
    return starts, listed


def dense_kernel(pieces, starts, listed, values, after, *rest):
    outs, total = rest[:-1], rest[-1]
    slot_count = listed.shape[0]

    def window(out, entry):
        wide = out.shape[1] // TILE
        place = (entry // slot_count) & 31
        u, v = place // wide, place & (wide - 1)
        return out.at[pl.ds(pl.multiple_of(u * TILE, TILE), TILE), pl.ds(pl.multiple_of(v * TILE, TILE), TILE)]

    for piece, out in zip(pieces, outs):

        def clear(i, carry):
            out[pl.ds(pl.multiple_of(i * 64, 64), 64), :] = jnp.zeros((64, out.shape[1]), bf16)
            return carry

        def place_first(j, carry):
            entry = listed[j]
            window(out, entry)[...] = values[entry & (slot_count - 1)]
            return carry

        def add(j, carry):
            entry = listed[j]
            cell = entry // slot_count
            spot = window(out, entry)
            base = jnp.where(cell == carry, total[...], spot[...].astype(f32))
            value = base + values[entry & (slot_count - 1)].astype(f32)
            total[...] = value
            spot[...] = value.astype(bf16)
            return cell

        lax.fori_loop(0, out.shape[0] // 64, clear, 0)
        lax.fori_loop(starts[piece], starts[piece + 1], place_first, 0)
        again = REPEATS // 32 + piece
        lax.fori_loop(starts[again], starts[again + 1], add, -1)


VMEM = pl.BlockSpec(memory_space=pltpu.VMEM)
SMEM = pl.BlockSpec(memory_space=pltpu.SMEM)


def dense_pieces(pieces, starts, listed, values, after):
    shapes = [
        jax.ShapeDtypeStruct((NC * TILE, (NZ if p < NY else NY) * TILE), bf16)
        for p in pieces
    ]
    return pl.pallas_call(
        functools.partial(dense_kernel, pieces),
        out_shape=shapes,
        in_specs=[SMEM, SMEM, VMEM, pl.BlockSpec(memory_space=pl.ANY)],
        out_specs=[VMEM] * len(pieces),
        scratch_shapes=[pltpu.VMEM((TILE, TILE), f32)],
        compiler_params=pltpu.CompilerParams(vmem_limit_bytes=4 * 2**20),
        cost_estimate=pl.CostEstimate(flops=4 * 10**6, bytes_accessed=10 * 2**20, transcendentals=0),
        name=f"dense{pieces[0]}",
    )(starts, listed, values, after)


def last_dot_kernel(so_far, weights, near, far, *outs):
    half = near.shape[0]
    for k, out in enumerate(outs, 1):
        rows = slice(k * TILE, (k + 1) * TILE)
        out[...] = (
            so_far[rows, :] + dot(weights[rows, :half], near[...]) + dot(weights[rows, half:], far[...])
        ).astype(out.dtype)


def last_dot(so_far, weights, near, far, types):
    shape = (TILE, so_far.shape[1])
    return pl.pallas_call(
        last_dot_kernel,
        out_shape=[jax.ShapeDtypeStruct(shape, t) for t in types],
        in_specs=[VMEM] * 4,
        out_specs=[VMEM] * len(types),
        compiler_params=pltpu.CompilerParams(vmem_limit_bytes=8 * 2**20),
        cost_estimate=pl.CostEstimate(flops=3 * 10**8, bytes_accessed=2 * 2**20, transcendentals=0),
        name="last_dot",
    )(so_far, weights, near, far)


def middle_kernel(scale, place, divisor, *rest):
    inputs, (layer_out, grad_pre), rest = rest[:8], rest[8:10], rest[10:]
    packets, held, (local, layer_held, sems) = rest[:NC], rest[NC : NC + 8], rest[NC + 8 :]
    copies = [
        pltpu.make_async_copy(source, target, sems.at[i])
        for i, (source, target) in enumerate(zip(inputs, held))
    ]
    for copy in copies:
        copy.start()
    for copy in copies:
        copy.wait()
    own, got1, got2, got3, self_part, features, w_neigh, grad_out = held
    nodes, width = features.shape
    agg_sum = own[...] + got1[...] + got2[...].astype(f32) + got3[...].astype(f32)
    aggregate = (agg_sum / divisor[...]).astype(bf16)
    pre_act = self_part[...] + dot(aggregate, w_neigh[...])
    sigmoid_pre = jax.nn.sigmoid(pre_act)
    layer_held[...] = (pre_act * sigmoid_pre).astype(bf16)
    leave = pltpu.make_async_copy(layer_held, layer_out, sems.at[8])
    leave.start()
    grad = (
        grad_out[...].astype(f32) * (sigmoid_pre * (1.0 + pre_act * (1.0 - sigmoid_pre)))
    ).astype(bf16)
    grad_pre[...] = grad
    back = lax.dot_general(
        grad, w_neigh[...], (((1,), (1,)), ((), ())), preferred_element_type=f32
    )
    scaled = (back / divisor[...]).astype(bf16)
    local[:width, :] = (dot_t(features[...], grad) * scale).astype(bf16)
    local[width:, :] = (dot_t(aggregate, grad) * scale).astype(bf16)
    bias = jnp.sum(grad.astype(f32), axis=0, keepdims=True) * scale
    bias = jnp.where(lax.broadcasted_iota(jnp.int32, (16, width), 0) == 0, bias, 0.0).astype(bf16)
    for k, packet in enumerate(packets):
        packet[:nodes, :] = scaled
        start = pl.multiple_of((place[0] ^ k) * nodes, nodes)
        packet[nodes : 2 * nodes, :] = local[pl.ds(start, nodes), :]
        packet[2 * nodes :, :] = bias
    leave.wait()


def middle(scale, place, divisor, sums, self_part, features, w_neigh, grad_out):
    nodes, width = features.shape
    inputs = [*sums, self_part, features, w_neigh, grad_out]
    node_shape = jax.ShapeDtypeStruct((nodes, width), bf16)
    packet_shape = jax.ShapeDtypeStruct((2 * nodes + 16, width), bf16)
    anywhere = pl.BlockSpec(memory_space=pl.ANY)
    return pl.pallas_call(
        functools.partial(middle_kernel, scale),
        out_shape=[node_shape] * 2 + [packet_shape] * NC,
        in_specs=[SMEM, VMEM] + [anywhere] * 8,
        out_specs=[anywhere, VMEM] + [VMEM] * NC,
        scratch_shapes=[pltpu.VMEM(a.shape, a.dtype) for a in inputs]
        + [
            pltpu.VMEM((2 * width, width), bf16),
            pltpu.VMEM((nodes, width), bf16),
            pltpu.SemaphoreType.DMA((9,)),
        ],
        compiler_params=pltpu.CompilerParams(vmem_limit_bytes=8 * 2**20),
        cost_estimate=pl.CostEstimate(flops=10**8, bytes_accessed=2 * 2**20, transcendentals=nodes * width),
        name="middle",
    )(place, divisor, *inputs)


def dot(a, b):
    return jnp.dot(a, b, preferred_element_type=f32)


def dot_t(a, b):
    return lax.dot_general(a, b, (((0,), (0,)), ((), ())), preferred_element_type=f32)


def add_up(parts):
    parts = [p.astype(f32) for p in parts]
    while len(parts) > 1:
        half = len(parts) // 2
        parts = [a + b for a, b in zip(parts[:half], parts[half:])]
    return parts[0]


def shards(
    features,
    degree,
    tile_count,
    tile_rows,
    tile_cols,
    tile_values,
    w_self,
    w_neigh,
    bias_term,
    grad_out,
):
    r, c = lax.axis_index("row"), lax.axis_index("col")
    x = r // NZ % NX
    nodes, width = features.shape
    node_total = nodes * NY * NX * NZ * NC

    starts, listed = plan_tiles(tile_count, tile_rows, tile_cols)
    values = tile_values[0, 0]

    other = swap_x(features)
    block0 = jnp.where(x == 0, features, other)
    block1 = jnp.where(x == 0, other, features)
    down1, up1 = shift_z(block0, 1), shift_z(block0, -1)
    line_y = jnp.concatenate(
        [block1, shift_y(block1, 1), shift_y(block1, -1), shift_y(block1, 2)], axis=0
    )
    size = line_y.shape[0]
    line_a = jnp.concatenate([block0, down1, up1], axis=0)
    down2 = shift_z(jnp.concatenate([line_y, down1], axis=0), 1)
    up2 = shift_z(jnp.concatenate([line_y, up1], axis=0), -1)
    down3, up3 = shift_z(down2, 1), shift_z(up2, -1)
    far = shift_z(down2[size:], 2)
    line_b = jnp.concatenate(
        [down2[size:], up2[size:], down3[size:], up3[size:], far], axis=0
    )
    cut, half = line_a.shape[0], NZ // 2 * nodes
    down_a, up_a = shift_y(line_a, 1), shift_y(line_a, -1)
    down_b, up_b = shift_y(line_b, 1), shift_y(line_b, -1)
    far = (
        shift_y(jnp.concatenate([down_a, down_b[: half - cut]], axis=0), 1),
        shift_y(up_b[half - cut :], -1),
    )
    down4, up4 = shift_z(down3[:size], 1), shift_z(up3[:size], -1)
    down5 = shift_z(down4, 1)
    plane_z = [line_y, down2[:size], up2[:size], down3[:size], up3[:size], down4, up4, down5]
    dense_z = dense_pieces(range(NY, PIECES), starts, listed, values, up2)
    dense_y = dense_pieces(range(NY), starts, listed, values, up_a)

    so_far = None
    pairs = [(dense_y[i][:, :cut], block) for i, block in enumerate((line_a, down_a, up_a))]
    pairs += [(dense_y[i][:, cut:], block) for i, block in enumerate((line_b, down_b, up_b))]
    for a, b in pairs + list(zip(dense_z, plane_z)):
        so_far = dot(a, b) if so_far is None else so_far + dot(a, b)
    sent = last_dot(so_far, dense_y[3], *far, [f32, bf16, bf16])
    sums = [swap_col(block, k) for k, block in enumerate(sent, 1)]
    own = so_far[:nodes] + dot(dense_y[3][:nodes], jnp.concatenate(far, axis=0))
    sums = [own, *sums]

    divisor = degree[:, None].astype(f32)
    self_part = dot(features, w_self) + bias_term
    layer_out, grad_pre, *packets = middle(
        1.0 / math.sqrt(node_total),
        jnp.reshape(c, (1,)),
        divisor,
        sums,
        self_part,
        features,
        w_neigh,
        grad_out,
    )
    packets = [packets[0]] + [swap_col(packets[k], k) for k in range(1, NC)]
    row_grads = jnp.concatenate([p[:nodes] for p in packets], axis=0)
    rider = add_up([p[nodes:] for p in packets])
    rider = (rider + swap_x(rider)).astype(bf16)

    def message(*blocks):
        return jnp.concatenate([block.astype(bf16) for block in blocks], axis=0)

    far = dot_t(dense_y[3], row_grads)
    down, up = message(far[:half]), message(far[half:])
    down, up, row_grads = lax.optimization_barrier((down, up, row_grads))
    down, up = shift_y(down, 1).astype(f32), shift_y(up, -1).astype(f32)
    terms_y = [dot_t(a, row_grads) for a in dense_y[:3]]
    top, down = down[:cut], down[cut:]
    before, after = terms_y[1], terms_y[2]
    down_b = message(after[cut:half] + down, after[half:], rider)
    up_b = message(before[cut:half], before[half:] + up, rider)
    down_b, up_b, late, late_rider = lax.optimization_barrier((down_b, up_b, row_grads, rider))
    terms_z = [dot_t(a, late if i in (5, 6) else row_grads) for i, a in enumerate(dense_z)]
    down_b, up_b = shift_y(down_b, 1), shift_y(up_b, -1)
    down_b, up_b, top, rest = lax.optimization_barrier(
        (down_b, up_b, message(after[:cut] + top), message(before[:cut]))
    )
    down_a, up_a = shift_y(top, 1), shift_y(rest, -1)
    wide = NZ * nodes - cut
    rider = add_up([rider, up_b[wide:], shift_y(late_rider, 2), down_b[wide:]]).astype(bf16)
    back_z = [
        terms_y[0][:cut] + down_a.astype(f32) + up_a.astype(f32),
        terms_y[0][cut:] + down_b[:wide].astype(f32) + up_b[:wide].astype(f32),
    ]
    back_z = [part[i : i + nodes] for part in back_z for i in range(0, part.shape[0], nodes)]

    ring1 = shift_z(message(terms_z[7]), 1).astype(f32)
    down2 = shift_z(message(terms_z[6] + ring1), 1).astype(f32)
    up2 = shift_z(message(terms_z[5]), -1).astype(f32)
    down3 = shift_z(message(terms_z[4] + down2, back_z[6], rider), 1)
    up3 = shift_z(message(terms_z[3] + up2, back_z[5], rider), -1)
    far = shift_z(message(back_z[7]), 2).astype(f32)

    down3, up3 = lax.optimization_barrier((down3, up3))

    def split(got):
        return got[:size].astype(f32), got[size : size + nodes].astype(f32), got[size + nodes :]

    ring_d, block_d, rider_d1 = split(down3)
    ring_u, block_u, rider_u1 = split(up3)
    down4 = shift_z(message(terms_z[2] + ring_d, back_z[4] + block_d + far, rider_d1), 1)
    up4 = shift_z(message(terms_z[1] + ring_u, back_z[3] + block_u, rider_u1), -1)
    down4, up4 = lax.optimization_barrier((down4, up4))
    ring_d, block_d, rider_d2 = split(down4)
    ring_u, block_u, rider_u2 = split(up4)
    rider4 = shift_z(rider_d2, 2)
    back_y = terms_z[0] + ring_d + ring_u
    down5 = shift_z(message(back_z[2] + block_d, rider_d2), 1)
    up5 = shift_z(message(back_z[1] + block_u, rider_u2), -1)
    sum0 = back_z[0] + down5[:nodes].astype(f32) + up5[:nodes].astype(f32)
    rider_d3, rider_u3 = down5[nodes:], up5[nodes:]
    sum1 = back_y[:nodes]
    for i, d in enumerate(OFFSETS_Y[1:], 1):
        sum1 = sum1 + shift_y(message(back_y[i * nodes : (i + 1) * nodes]), d).astype(f32)

    total = add_up(
        [rider, rider_u1, rider_u2, rider_u3, rider4, rider_d3, rider_d2, rider_d1]
    )
    quarter = total[:nodes].astype(bf16)
    quarters = jnp.stack([quarter] + [swap_col(quarter, k) for k in range(1, NC)])
    grads = quarters[c ^ jnp.arange(NC, dtype=jnp.int32)].reshape(NC * nodes, width).astype(f32)

    kept = jnp.where(x == 0, sum0, sum1)
    sent = jnp.where(x == 0, sum1, sum0)
    neighbor_back = kept + swap_x(sent)
    grad_input = (dot(grad_pre, w_self.T) + neighbor_back).astype(bf16)
    return (layer_out, grad_input, grads[:width], grads[width:], total[nodes])


def solution(mesh):
    return jax.shard_map(
        shards,
        mesh=mesh,
        in_specs=(
            P(("row", "col"), None),
            P(("row", "col")),
            P("col", "row"),
            P("col", "row", None),
            P("col", "row", None),
            P("col", "row", None, None, None),
            P(),
            P(),
            P(),
            P(("row", "col"), None),
        ),
        out_specs=(P(("row", "col"), None), P(("row", "col"), None), P(), P(), P()),
        check_vma=False,
    )
```
